32 devices in a mesh: seq: 8 (over z, core), head: 4 (over y, x).
Axes of the slice: x: 2, y: 2, z: 4, core: 2. Of those that a mesh axis runs over, the one named last changes fastest.
Arguments:
- queries: bfloat16 [1024, 4096], P(('seq', 'head')), as said below
- keys: bfloat16 [1024, 4096], P('seq', 'head'), as said below
- values: bfloat16 [1024, 4096], P('seq', 'head'), may hold values from -6 to 6
- block_order: int32 [8], replicated, may hold values from 0 to 7, each once
Outputs:
- attended: bfloat16 [1024, 4096], P('seq', 'head')
The draws below stay inside these ranges and needn't reach their ends.
Inputs may be any that keep to these rules, and one draw needn't show every extreme that they name: `block_order`: each storage block holds a different sequence block. `queries`: entries lie within -8 to 8. `keys`: entries lie within -8 to 8.
All inputs are finite; a program needn't handle non-finite values.
Results may differ from the reference program's by a relative error of at most 0.006.
Values may be sent and summed in bfloat16 or wider, within the bound.
No kernel may reach another device: no remote copies, remote signals or barrier semaphores. Data moves between devices by JAX's collectives and lax.ppermute only.
A program may use at most 64 MiB of HBM per device.

```python
import jax
import jax.numpy as jnp
from jax import lax

HEADS = 32
HEAD_DIM = 128
TOK_DEV = 128
SEQ_BLOCKS = 8
TOKENS = 1024


def shared_pair(key):
    tokens = TOK_DEV * SEQ_BLOCKS
    width = HEADS * HEAD_DIM
    key_a, key_b = jax.random.split(key, 2)
    q_all = jnp.clip(jax.random.normal(key_a, (tokens, width), jnp.float32), -6.0, 6.0)
    k_all = jnp.clip(jax.random.normal(key_b, (tokens, width), jnp.float32), -6.0, 6.0)
    return (q_all, k_all)


def draw_queries(key, part):
    q_all, k_all = shared_pair(jax.random.fold_in(key, 7))
    return q_all.astype(jnp.bfloat16)


def draw_keys(key, part):
    q_all, k_all = shared_pair(jax.random.fold_in(key, 7))
    return k_all.astype(jnp.bfloat16)


def shard_levels(rng, dims, shards, smallest, top_value):
    def one(axis_at, blocks):
        heights = jax.random.uniform(jax.random.fold_in(jax.random.fold_in(rng, 6), axis_at), (blocks,), jnp.float32, smallest / len(shards), top_value / len(shards))
        return jnp.repeat(jnp.exp(heights), dims[axis_at] // blocks).reshape((-1,) + (1,) * (len(dims) - axis_at - 1))

    loudness = one(*shards[0])
    for cut in shards[1:]:
        loudness = loudness * one(*cut)
    return loudness


def normal_values(stream_key, extent, scale, reach, shards=(), kind=jnp.bfloat16):
    values = jax.random.normal(stream_key, extent, jnp.float32) * scale
    if len(shards) > 0:
        values = shard_levels(stream_key, extent, shards, -0.22, 0.18) * values
    return jnp.clip(values, min=-reach, max=reach).astype(kind)


def setup_inputs(seed: int = 0) -> dict:
    arg_keys = jax.random.split(jax.random.key(seed), 5)
    return {
        "queries": draw_queries(jax.random.fold_in(arg_keys[4], 71), 0),
        "keys": draw_keys(jax.random.fold_in(arg_keys[4], 71), 0),
        "values": normal_values(arg_keys[2], (TOKENS, HEADS * HEAD_DIM), 1.0, 6.0, ((0, 8), (1, 4))),
        "block_order": jax.random.permutation(arg_keys[3], SEQ_BLOCKS).astype(jnp.int32),
    }


def reference(queries, keys, values, block_order):
    tokens = queries.shape[0]
    rows = jnp.arange(tokens, dtype=jnp.int32)
    positions = (block_order[rows // TOK_DEV] * TOK_DEV + rows % TOK_DEV).astype(jnp.int32)
    scale = 1.0 / (HEAD_DIM ** 0.5)
    q_heads = jnp.transpose(queries.reshape(tokens, HEADS, HEAD_DIM), (1, 0, 2))
    k_heads = jnp.transpose(keys.reshape(tokens, HEADS, HEAD_DIM), (1, 0, 2))
    v_heads = jnp.transpose(values.reshape(tokens, HEADS, HEAD_DIM), (1, 0, 2))
    block = 512 if tokens % 512 == 0 else tokens
    q_pos = positions.reshape(tokens // block, block)

    def one_head(operands):
        q_one, k_one, v_one = operands
        q_blocks = q_one.reshape(tokens // block, block, HEAD_DIM)

        def one_block(pieces):
            q_block, pos_block = pieces
            scores = jnp.dot(q_block, k_one.T, preferred_element_type=jnp.float32) * scale
            allowed = positions[None, :] <= pos_block[:, None]
            scores = jnp.where(allowed, scores, jnp.float32(-1e30))
            rowmax = jnp.max(scores, axis=1, keepdims=True)
            weight = jnp.where(allowed, jnp.exp(scores - rowmax), jnp.float32(0.0))
            total = jnp.sum(weight, axis=1, keepdims=True)
            mixed = jnp.dot(weight.astype(jnp.bfloat16), v_one, preferred_element_type=jnp.float32)
            return mixed / total

        out = lax.map(one_block, (q_blocks, q_pos))
        return out.reshape(tokens, HEAD_DIM)

    result = lax.map(one_head, (q_heads, k_heads, v_heads))
    return jnp.transpose(result, (1, 0, 2)).reshape(tokens, HEADS * HEAD_DIM).astype(jnp.bfloat16)
```

```python
import functools

import jax
import jax.numpy as jnp
from jax import lax
from jax.experimental import pallas as pl
from jax.experimental.pallas import tpu as pltpu
from jax.sharding import PartitionSpec as P

HEAD_DIM = 128
CORES = 2
LOG2E = 1.4426950408889634
ANY = pl.BlockSpec(memory_space=pl.ANY)
HBM = pl.BlockSpec(memory_space=pltpu.HBM)
VMEM = pl.BlockSpec(memory_space=pltpu.VMEM)
SMEM = pl.BlockSpec(memory_space=pltpu.SMEM)
PARAMS = pltpu.CompilerParams(vmem_limit_bytes=16 * 2**20)


def shifted(block, axis, distance):
    devices = range(lax.axis_size(axis))
    route = [((i - distance) % len(devices), i) for i in devices]
    return lax.ppermute(block, axis, route)


def swapped(block, axis, bits):
    route = [(i, i ^ bits) for i in range(lax.axis_size(axis))]
    return lax.ppermute(block, axis, route)


def place():
    me = lax.axis_index("seq")
    return me // CORES, me % CORES, lax.axis_index("head")


def cut(start, size):
    return pl.ds(pl.multiple_of(start * size, size), size)


def split_kernel(chips, q_ref, k_ref, v_ref, *rest):
    kv_refs, q_refs, sem = rest[:chips], rest[chips:-1], rest[-1]
    z, _, head = place()
    width = k_ref.shape[1] // chips
    copies = []

    def copy(source, target):
        copies.append(pltpu.make_async_copy(source, target, sem.at[len(copies)]))
        copies[-1].start()

    for step in list(range(1, chips)) + [0]:
        copy(k_ref.at[:, cut(z ^ step, width)], kv_refs[step].at[:, pl.ds(0, width)])
        copy(v_ref.at[:, cut(z ^ step, width)], kv_refs[step].at[:, pl.ds(width, width)])
    for turn, target in enumerate(q_refs):
        copy(q_ref.at[:, cut(head ^ turn, target.shape[1])], target)
    for one in copies:
        one.wait()


def split(queries, keys, values, chips):
    rows, width = keys.shape
    groups = queries.shape[1] // width
    part = width // chips
    outs = [jax.ShapeDtypeStruct((rows, 2 * part), keys.dtype)] * chips
    outs += [jax.ShapeDtypeStruct((queries.shape[0], width), queries.dtype)] * groups
    outs = pl.pallas_call(
        functools.partial(split_kernel, chips),
        out_shape=outs,
        in_specs=[HBM] * 3,
        out_specs=[ANY] * len(outs),
        scratch_shapes=[pltpu.SemaphoreType.DMA((2 * chips + groups,))],
        compiler_params=PARAMS,
    )(queries, keys, values)
    return outs[:chips], outs[chips:]


def regroup_kernel(chips, groups, order_ref, *rest):
    parts, outs, rel_ref, sem = rest[:groups], rest[groups:-2], rest[-2], rest[-1]
    z, core, head = place()
    sub, width = parts[0].shape[0], outs[0].shape[1]
    copies = []
    for step, out in enumerate(outs):
        for turn, part in enumerate(parts):
            copies.append(
                pltpu.make_async_copy(
                    part.at[:, cut(z ^ step, width)],
                    out.at[cut(head ^ turn, sub), :],
                    sem.at[len(copies)],
                )
            )
            copies[-1].start()
    rows = rel_ref.shape[2] // (chips * CORES)
    inner = lax.broadcasted_iota(jnp.int32, (8, rows), 1)
    for step in range(chips):
        mine = order_ref[(z ^ step) * CORES + core]
        for slot in range(chips * CORES):
            block = (z ^ (slot // CORES)) * CORES + (core ^ (slot % CORES))
            rel_ref[step, :, pl.ds(slot * rows, rows)] = inner + (order_ref[block] - mine) * rows
    for one in copies:
        one.wait()


def regroup(block_order, parts, rows, chips):
    groups, width = len(parts), parts[0].shape[1] // chips
    outs = [jax.ShapeDtypeStruct((rows, width), parts[0].dtype)] * chips
    outs += [jax.ShapeDtypeStruct((chips, 8, rows * chips * CORES), jnp.int32)]
    outs = pl.pallas_call(
        functools.partial(regroup_kernel, chips, groups),
        out_shape=outs,
        in_specs=[SMEM] + [ANY] * groups,
        out_specs=[ANY] * chips + [VMEM],
        scratch_shapes=[pltpu.SemaphoreType.DMA((chips * groups,))],
        compiler_params=PARAMS,
    )(block_order, *parts)
    return outs[:chips], outs[chips]


def attend_kernel(step, rel_ref, q_ref, *rest):
    kv_refs, out = rest[:-1], rest[-1]
    rows, width = out.shape
    scale = LOG2E / HEAD_DIM**0.5
    below = lax.broadcasted_iota(jnp.int32, (rows, 2 * rows), 0)
    for one in range(width // HEAD_DIM):
        cols = pl.ds(one * HEAD_DIM, HEAD_DIM)
        scores = []
        for pair in range(0, len(kv_refs), 2):
            k = jnp.concatenate([r[:, cols] for r in kv_refs[pair : pair + 2]], 0)
            s = lax.dot_general(q_ref[:, cols], k, (((1,), (1,)), ((), ())), preferred_element_type=jnp.float32)
            rel = rel_ref[step, 0:1, pl.ds(pair * rows, 2 * rows)]
            scores.append(jnp.where(rel <= below, s, jnp.float32(-1e30)))
        top = jnp.max(functools.reduce(jnp.maximum, scores), axis=1, keepdims=True)
        total = jnp.zeros((rows, 1), jnp.float32)
        mixed = jnp.zeros((rows, HEAD_DIM), jnp.float32)
        cols = pl.ds(width + one * HEAD_DIM, HEAD_DIM)
        for pair in range(0, len(kv_refs), 2):
            weight = jnp.exp2((scores[pair // 2] - top) * scale)
            total += jnp.sum(weight, axis=1, keepdims=True)
            v = jnp.concatenate([r[:, cols] for r in kv_refs[pair : pair + 2]], 0)
            mixed += jnp.dot(weight.astype(jnp.bfloat16), v, preferred_element_type=jnp.float32)
        out[:, pl.ds(one * HEAD_DIM, HEAD_DIM)] = (mixed / total).astype(out.dtype)


def attend(step, rel, q, kv):
    return pl.pallas_call(
        functools.partial(attend_kernel, step),
        out_shape=jax.ShapeDtypeStruct(q.shape, q.dtype),
        in_specs=[VMEM] * (2 + len(kv)),
        out_specs=VMEM,
        compiler_params=PARAMS,
    )(rel, q, *kv)


def join_kernel(chips, *refs):
    parts, out, sem = refs[:chips], refs[chips], refs[-1]
    z, _, _ = place()
    width = parts[0].shape[1]
    copies = []
    for step in range(chips):
        copies.append(
            pltpu.make_async_copy(parts[step], out.at[:, cut(z ^ step, width)], sem.at[step])
        )
        copies[-1].start()
    for one in copies:
        one.wait()


def join(parts):
    chips = len(parts)
    rows, width = parts[0].shape
    return pl.pallas_call(
        functools.partial(join_kernel, chips),
        out_shape=jax.ShapeDtypeStruct((rows, width * chips), parts[0].dtype),
        in_specs=[ANY] * chips,
        out_specs=ANY,
        scratch_shapes=[pltpu.SemaphoreType.DMA((chips,))],
        compiler_params=PARAMS,
    )(*parts)


def by_heads(queries, keys, values, block_order):
    chips = lax.axis_size("seq") // CORES
    groups = lax.axis_size("head")
    rows = keys.shape[0]
    far_first = sorted(range(1, chips), key=lambda step: step < chips // 2)
    kv_cut, q_cut = split(queries, keys, values, chips)
    near, far, q_got, out = {0: kv_cut[0]}, {}, {}, {}
    for step in far_first:
        near[step] = swapped(kv_cut[step], "seq", CORES * step)
    q_parts = [q_cut[0]] + [swapped(q_cut[turn], "head", turn) for turn in range(1, groups)]
    q_chips, rel = regroup(block_order, q_parts, rows, chips)
    for step in far_first:
        q_got[step] = swapped(q_chips[step], "seq", CORES * step)
    kv = []
    for step in range(chips):
        kv += [near[step], swapped(near[step], "seq", 1)]
    for step in far_first:
        out[step] = swapped(attend(step, rel, q_got[step], kv), "seq", CORES * step)
    out[0] = attend(0, rel, q_chips[0], kv)
    return join([out[step] for step in range(chips)])


def around_ring(queries, keys, values, block_order):
    seq_count = lax.axis_size("seq")
    me_index = lax.axis_index("seq")
    local_q = lax.all_to_all(queries, "head", split_axis=1, concat_axis=0, tiled=True)
    rows = local_q.shape[0]
    head_count = local_q.shape[1] // HEAD_DIM
    q_three = local_q.reshape(rows, head_count, HEAD_DIM)
    mine = block_order[me_index]
    scale = 1.0 / HEAD_DIM**0.5

    def tile(state, kv_pair, allowed):
        rowmax, total, accum = state
        key_count = kv_pair[0].shape[0]
        k_three = kv_pair[0].reshape(key_count, head_count, HEAD_DIM)
        v_three = kv_pair[1].reshape(key_count, head_count, HEAD_DIM)
        scores = (
            jnp.einsum("qhd,khd->hqk", q_three, k_three, preferred_element_type=jnp.float32) * scale
        )
        scores = jnp.where(allowed[None], scores, jnp.float32(-1e30))
        new_max = jnp.maximum(rowmax, jnp.max(scores, axis=2))
        factor = jnp.exp(rowmax - new_max)
        weight = jnp.where(allowed[None], jnp.exp(scores - new_max[:, :, None]), jnp.float32(0.0))
        total = total * factor + jnp.sum(weight, axis=2)
        mixed = jnp.einsum(
            "hqk,khd->qhd", weight.astype(jnp.bfloat16), v_three, preferred_element_type=jnp.float32
        )
        accum = accum * jnp.transpose(factor)[:, :, None] + mixed
        return (new_max, total, accum)

    def absorb(state, kv_pair, source):
        visible = block_order[source % seq_count] < mine
        allowed = jnp.broadcast_to(visible, (rows, rows))
        return tile(state, kv_pair, allowed)

    start_state = (
        jnp.full((head_count, rows), -1e30, jnp.float32),
        jnp.zeros((head_count, rows), jnp.float32),
        jnp.zeros((rows, head_count, HEAD_DIM), jnp.float32),
    )
    query_idx = lax.broadcasted_iota(jnp.int32, (rows, rows), 0)
    key_idx = lax.broadcasted_iota(jnp.int32, (rows, rows), 1)
    state = tile(start_state, (keys, values), key_idx <= query_idx)

    def both_turn(step, carry):
        ahead, behind, st = carry
        ahead = tuple(shifted(part, "seq", 1) for part in ahead)
        st = absorb(st, ahead, me_index - step + seq_count)
        behind = tuple(shifted(part, "seq", -1) for part in behind)
        st = absorb(st, behind, me_index + step)
        return (ahead, behind, st)

    ahead, behind, state = lax.fori_loop(
        1, (seq_count - 1) // 2 + 1, both_turn, ((keys, values), (keys, values), state)
    )
    if seq_count % 2 == 0:
        ahead = tuple(shifted(part, "seq", 1) for part in ahead)
        state = absorb(state, ahead, me_index - seq_count // 2 + seq_count)
    rowmax, total, accum = state
    result = accum / jnp.transpose(total)[:, :, None]
    return result.reshape(rows, head_count * HEAD_DIM).astype(jnp.bfloat16)


def body(queries, keys, values, block_order):
    seq_count, groups = lax.axis_size("seq"), lax.axis_size("head")
    chips = seq_count // CORES
    heads = keys.shape[1] // HEAD_DIM
    powers = all(n > 1 and n & (n - 1) == 0 for n in (chips, groups))
    if seq_count % CORES == 0 and powers and heads % chips == 0:
        return by_heads(queries, keys, values, block_order)
    return around_ring(queries, keys, values, block_order)


def solution(mesh):
    in_specs = (P(("seq", "head"), None), P("seq", "head"), P("seq", "head"), P())
    out_specs = P("seq", "head")
    return jax.shard_map(body, mesh=mesh, in_specs=in_specs, out_specs=out_specs, check_vma=False)
```

```python
import functools

import jax
import jax.numpy as jnp
from jax import lax
from jax.experimental import pallas as pl
from jax.experimental.pallas import tpu as pltpu
from jax.sharding import PartitionSpec as P

HEAD_DIM = 128
CORES = 2
LOG2E = 1.4426950408889634
ANY = pl.BlockSpec(memory_space=pl.ANY)
HBM = pl.BlockSpec(memory_space=pltpu.HBM)
VMEM = pl.BlockSpec(memory_space=pltpu.VMEM)
SMEM = pl.BlockSpec(memory_space=pltpu.SMEM)
PARAMS = pltpu.CompilerParams(vmem_limit_bytes=16 * 2**20)
STACK_COST = pl.CostEstimate(flops=20 * 10**9, bytes_accessed=0, transcendentals=0)
NEAR_COST = pl.CostEstimate(flops=60 * 10**9, bytes_accessed=0, transcendentals=0)


def shifted(block, axis, distance):
    devices = range(lax.axis_size(axis))
    route = [((i - distance) % len(devices), i) for i in devices]
    return lax.ppermute(block, axis, route)


def swapped(block, axis, bits):
    route = [(i, i ^ bits) for i in range(lax.axis_size(axis))]
    return lax.ppermute(block, axis, route)


def place():
    me = lax.axis_index("seq")
    return me // CORES, me % CORES, lax.axis_index("head")


def over(block, turn):
    return swapped(block, "seq", CORES * turn)


def cut(start, size):
    return pl.ds(pl.multiple_of(start * size, size), size)


def copy_all(pairs, sem):
    copies = [pltpu.make_async_copy(one, other, sem.at[i]) for i, (one, other) in enumerate(pairs)]
    for one in copies:
        one.start()
    return copies


def cut_pairs(k_ref, v_ref, chip, out):
    width = out.shape[1] // 2
    return [
        (k_ref.at[:, cut(chip, width)], out.at[:, pl.ds(0, width)]),
        (v_ref.at[:, cut(chip, width)], out.at[:, pl.ds(width, width)]),
    ]


def split_kernel(chips, q_ref, k_ref, v_ref, *rest):
    kv_refs, q_refs, sem = rest[:chips], rest[chips:-1], rest[-1]
    z, _, head = place()
    pairs = []
    for turn in [*range(1, chips), 0]:
        pairs += cut_pairs(k_ref, v_ref, z ^ turn, kv_refs[turn])
    for step, out in enumerate(q_refs):
        pairs.append((q_ref.at[:, cut(head ^ step, out.shape[1])], out))
    for one in copy_all(pairs, sem):
        one.wait()


def split(queries, keys, values, chips):
    rows, width = keys.shape
    groups = queries.shape[1] // width
    outs = [jax.ShapeDtypeStruct((rows, 2 * width // chips), keys.dtype)] * chips
    outs += [jax.ShapeDtypeStruct((queries.shape[0], width), queries.dtype)] * groups
    outs = pl.pallas_call(
        functools.partial(split_kernel, chips),
        out_shape=outs,
        in_specs=[HBM] * 3,
        out_specs=[ANY] * len(outs),
        scratch_shapes=[pltpu.SemaphoreType.DMA((2 * chips + groups,))],
        compiler_params=PARAMS,
    )(*(pltpu.with_memory_space_constraint(x, pltpu.HBM) for x in (queries, keys, values)))
    return outs[:chips], outs[chips:]


def regroup_kernel(chips, groups, order_ref, *rest):
    q_parts, q_refs, rel_ref = rest[:groups], rest[groups:-1], rest[-1]
    z, core, head = place()
    sub, (rows, width) = q_parts[0].shape[0], q_refs[0].shape
    for turn, out in enumerate(q_refs):
        for step, part in enumerate(q_parts):
            out[cut(head ^ step, sub), :] = part[:, cut(z ^ turn, width)]
    inner = lax.broadcasted_iota(jnp.int32, (8, rows), 1)
    starts = [
        order_ref[(z ^ (slot % chips)) * CORES + (core ^ (slot // chips))] * rows for slot in range(chips * CORES)
    ]
    for turn in range(chips):
        for slot, start in enumerate(starts):
            rel_ref[turn, :, pl.ds(slot * rows, rows)] = inner + (start - starts[turn])


def regroup(block_order, q_parts, rows, chips):
    outs = [jax.ShapeDtypeStruct((rows, q_parts[0].shape[1] // chips), q_parts[0].dtype)] * chips
    outs += [jax.ShapeDtypeStruct((chips, 8, rows * chips * CORES), jnp.int32)]
    outs = pl.pallas_call(
        functools.partial(regroup_kernel, chips, len(q_parts)),
        out_shape=outs,
        in_specs=[SMEM] + [VMEM] * len(q_parts),
        out_specs=[VMEM] * len(outs),
        compiler_params=PARAMS,
    )(block_order, *q_parts)
    return outs[:-1], outs[-1]


def stack_kernel(*refs):
    for at, ref in enumerate(refs[:-1]):
        refs[-1][at] = ref[...]


def stack(parts):
    return pl.pallas_call(
        stack_kernel,
        out_shape=jax.ShapeDtypeStruct((len(parts),) + parts[0].shape, parts[0].dtype),
        in_specs=[VMEM] * len(parts),
        out_specs=VMEM,
        compiler_params=PARAMS,
        cost_estimate=STACK_COST,
    )(*parts)


def attend_kernel(turns, count, first, stacked, alone, rel_ref, *rest):
    q_refs, rest = rest[: len(turns)], rest[len(turns) :]
    if first:
        blocks, states = rest[:count], rest[count:]
    else:
        blocks = {turn: rest[0].at[at] for at, turn in enumerate(stacked)} | dict(zip(alone, rest[1:]))
        blocks, rest = [blocks[turn] for turn in range(count)], rest[1 + len(alone) :]
        states, outs = rest[: 2 * len(turns)], rest[2 * len(turns) :]
    rows, width = q_refs[0].shape
    scale = LOG2E / HEAD_DIM**0.5
    below = lax.broadcasted_iota(jnp.int32, (rows, CORES * rows), 0)
    ones = jnp.ones((CORES * rows, HEAD_DIM), jnp.bfloat16)
    start = 0 if first else count * rows

    def both(at, column):
        return jnp.concatenate([ref[:, pl.ds(column, HEAD_DIM)] for ref in blocks[at : at + CORES]], 0)

    for index, (turn, q_ref) in enumerate(zip(turns, q_refs)):
        top_ref, sums_ref = states[2 * index : 2 * index + 2]
        for column in range(0, width, HEAD_DIM):
            tops, wide = pl.ds(column, HEAD_DIM), pl.ds(2 * column, 2 * HEAD_DIM)
            top = None if first else top_ref[:, tops]
            sums = None if first else sums_ref[:, wide]
            for at in range(0, count, CORES):
                s = lax.dot_general(
                    q_ref[:, tops], both(at, column), (((1,), (1,)), ((), ())), preferred_element_type=jnp.float32
                )
                rel = rel_ref[turn, 0:1, pl.ds(start + at * rows, CORES * rows)]
                s = jnp.where(rel <= below, s, jnp.float32(-1e30))
                high = jnp.broadcast_to(jnp.max(s, axis=1, keepdims=True), (rows, HEAD_DIM))
                high = high if top is None else jnp.maximum(top, high)
                weight = jnp.exp2((s - jnp.concatenate([high] * CORES, 1)) * scale).astype(jnp.bfloat16)
                values = jnp.concatenate([both(at, width + column), ones], 1)
                mixed = jnp.dot(weight, values, preferred_element_type=jnp.float32)
                if top is not None:
                    shrink = jnp.exp2((top - high) * scale)
                    mixed += sums * jnp.concatenate([shrink, shrink], 1)
                top, sums = high, mixed
            if first:
                top_ref[:, tops], sums_ref[:, wide] = top, sums
            else:
                outs[index][:, tops] = (sums[:, :HEAD_DIM] / sums[:, HEAD_DIM:]).astype(outs[index].dtype)


def attend_near(turns, rel, q, near):
    rows, width = q[0].shape
    state = [jax.ShapeDtypeStruct((rows, wide), jnp.float32) for wide in (width, 2 * width)]
    outs = pl.pallas_call(
        functools.partial(attend_kernel, turns, len(near), True, (), ()),
        out_shape=state * len(turns),
        in_specs=[VMEM] * (1 + len(turns) + len(near)),
        out_specs=[VMEM] * (2 * len(turns)),
        compiler_params=PARAMS,
        cost_estimate=NEAR_COST,
    )(rel, *(q[turn] for turn in turns), *near)
    return {turn: outs[2 * index : 2 * index + 2] for index, turn in enumerate(turns)}


def attend_far(turns, rel, q, far, stacked, alone, states):
    return pl.pallas_call(
        functools.partial(attend_kernel, turns, len(q), False, stacked, tuple(alone)),
        out_shape=[jax.ShapeDtypeStruct(q[0].shape, q[0].dtype)] * len(turns),
        in_specs=[VMEM] * (2 + len(alone) + 3 * len(turns)),
        out_specs=[VMEM] * len(turns),
        compiler_params=PARAMS,
    )(rel, *(q[turn] for turn in turns), far, *alone.values(), *(part for turn in turns for part in states[turn]))


def join_kernel(chips, *refs):
    parts, out, sem = refs[:chips], refs[-2], refs[-1]
    z, _, _ = place()
    width = parts[0].shape[1]
    pairs = [(part, out.at[:, cut(z ^ turn, width)]) for turn, part in enumerate(parts)]
    for one in copy_all(pairs, sem):
        one.wait()


def join(parts):
    chips, (rows, width) = len(parts), parts[0].shape
    return pl.pallas_call(
        functools.partial(join_kernel, chips),
        out_shape=jax.ShapeDtypeStruct((rows, width * chips), parts[0].dtype),
        in_specs=[ANY] * chips,
        out_specs=ANY,
        scratch_shapes=[pltpu.SemaphoreType.DMA((chips,))],
        compiler_params=PARAMS,
    )(*parts)


def by_heads(queries, keys, values, block_order):
    chips = lax.axis_size("seq") // CORES
    groups = lax.axis_size("head")
    half = chips // 2
    across, within = list(range(half, chips)), list(range(1, half))
    kv, q_cut = split(queries, keys, values, chips)
    near = [kv[0]] + [over(kv[turn], turn) for turn in range(1, chips)]
    q_parts = [q_cut[0]] + [swapped(q_cut[step], "head", step) for step in range(1, groups)]
    q, rel = regroup(block_order, q_parts, keys.shape[0], chips)
    q = [q[0]] + [over(q[turn], turn) for turn in range(1, chips)]
    stacked = [*across[::-1], 0]
    far = swapped(stack([near[turn] for turn in stacked]), "seq", 1)
    alone = {turn: swapped(near[turn], "seq", 1) for turn in within}
    states = attend_near([*across, *within, 0], rel, q, near)
    out = {}
    for turns in (across, [*within, 0]):
        for turn, part in zip(turns, attend_far(turns, rel, q, far, stacked, alone, states)):
            out[turn] = over(part, turn) if turn else part
    return join([out[turn] for turn in range(chips)])


def around_ring(queries, keys, values, block_order):
    seq_count = lax.axis_size("seq")
    me_index = lax.axis_index("seq")
    local_q = lax.all_to_all(queries, "head", split_axis=1, concat_axis=0, tiled=True)
    rows = local_q.shape[0]
    head_count = local_q.shape[1] // HEAD_DIM
    q_three = local_q.reshape(rows, head_count, HEAD_DIM)
    mine = block_order[me_index]
    scale = 1.0 / HEAD_DIM**0.5

    def tile(state, kv_pair, allowed):
        rowmax, total, accum = state
        key_count = kv_pair[0].shape[0]
        k_three = kv_pair[0].reshape(key_count, head_count, HEAD_DIM)
        v_three = kv_pair[1].reshape(key_count, head_count, HEAD_DIM)
        scores = (
            jnp.einsum("qhd,khd->hqk", q_three, k_three, preferred_element_type=jnp.float32) * scale
        )
        scores = jnp.where(allowed[None], scores, jnp.float32(-1e30))
        new_max = jnp.maximum(rowmax, jnp.max(scores, axis=2))
        factor = jnp.exp(rowmax - new_max)
        weight = jnp.where(allowed[None], jnp.exp(scores - new_max[:, :, None]), jnp.float32(0.0))
        total = total * factor + jnp.sum(weight, axis=2)
        mixed = jnp.einsum(
            "hqk,khd->qhd", weight.astype(jnp.bfloat16), v_three, preferred_element_type=jnp.float32
        )
        accum = accum * jnp.transpose(factor)[:, :, None] + mixed
        return (new_max, total, accum)

    def absorb(state, kv_pair, source):
        visible = block_order[source % seq_count] < mine
        allowed = jnp.broadcast_to(visible, (rows, rows))
        return tile(state, kv_pair, allowed)

    start_state = (
        jnp.full((head_count, rows), -1e30, jnp.float32),
        jnp.zeros((head_count, rows), jnp.float32),
        jnp.zeros((rows, head_count, HEAD_DIM), jnp.float32),
    )
    query_idx = lax.broadcasted_iota(jnp.int32, (rows, rows), 0)
    key_idx = lax.broadcasted_iota(jnp.int32, (rows, rows), 1)
    state = tile(start_state, (keys, values), key_idx <= query_idx)

    def both_turn(step, carry):
        ahead, behind, st = carry
        ahead = tuple(shifted(part, "seq", 1) for part in ahead)
        st = absorb(st, ahead, me_index - step + seq_count)
        behind = tuple(shifted(part, "seq", -1) for part in behind)
        st = absorb(st, behind, me_index + step)
        return (ahead, behind, st)

    ahead, behind, state = lax.fori_loop(
        1, (seq_count - 1) // 2 + 1, both_turn, ((keys, values), (keys, values), state)
    )
    if seq_count % 2 == 0:
        ahead = tuple(shifted(part, "seq", 1) for part in ahead)
        state = absorb(state, ahead, me_index - seq_count // 2 + seq_count)
    rowmax, total, accum = state
    result = accum / jnp.transpose(total)[:, :, None]
    return result.reshape(rows, head_count * HEAD_DIM).astype(jnp.bfloat16)


def body(queries, keys, values, block_order):
    seq_count, groups = lax.axis_size("seq"), lax.axis_size("head")
    chips = seq_count // CORES
    heads = keys.shape[1] // HEAD_DIM
    powers = all(n > 1 and n & (n - 1) == 0 for n in (chips, groups))
    if seq_count % CORES == 0 and powers and heads % chips == 0:
        return by_heads(queries, keys, values, block_order)
    return around_ring(queries, keys, values, block_order)


def solution(mesh):
    in_specs = (P(("seq", "head"), None), P("seq", "head"), P("seq", "head"), P())
    out_specs = P("seq", "head")
    return jax.shard_map(body, mesh=mesh, in_specs=in_specs, out_specs=out_specs, check_vma=False)
```

```python
import functools

import jax
import jax.numpy as jnp
from jax import lax
from jax.experimental import pallas as pl
from jax.experimental.pallas import tpu as pltpu
from jax.sharding import PartitionSpec as P

HEAD_DIM = 128
CORES = 2
LOG2E = 1.4426950408889634
ANY = pl.BlockSpec(memory_space=pl.ANY)
HBM = pl.BlockSpec(memory_space=pltpu.HBM)
VMEM = pl.BlockSpec(memory_space=pltpu.VMEM)
SMEM = pl.BlockSpec(memory_space=pltpu.SMEM)
PARAMS = pltpu.CompilerParams(vmem_limit_bytes=16 * 2**20)
STACK_COST = pl.CostEstimate(flops=20 * 10**9, bytes_accessed=0, transcendentals=0)
NEAR_COST = pl.CostEstimate(flops=60 * 10**9, bytes_accessed=0, transcendentals=0)


def shifted(block, axis, distance):
    devices = range(lax.axis_size(axis))
    route = [((i - distance) % len(devices), i) for i in devices]
    return lax.ppermute(block, axis, route)


def swapped(block, axis, bits):
    route = [(i, i ^ bits) for i in range(lax.axis_size(axis))]
    return lax.ppermute(block, axis, route)


def place():
    me = lax.axis_index("seq")
    return me // CORES, me % CORES, lax.axis_index("head")


def over(block, turn):
    return swapped(block, "seq", CORES * turn)


def cut(start, size):
    return pl.ds(pl.multiple_of(start * size, size), size)


def copy_all(pairs, sem):
    copies = [pltpu.make_async_copy(one, other, sem.at[i]) for i, (one, other) in enumerate(pairs)]
    for one in copies:
        one.start()
    return copies


def cut_pairs(k_ref, v_ref, chip, out):
    width = out.shape[1] // 2
    return [
        (k_ref.at[:, cut(chip, width)], out.at[:, pl.ds(0, width)]),
        (v_ref.at[:, cut(chip, width)], out.at[:, pl.ds(width, width)]),
    ]


def split_kernel(chips, q_ref, k_ref, v_ref, *rest):
    kv_refs, q_refs, sem = rest[:chips], rest[chips:-1], rest[-1]
    z, _, head = place()
    pairs = []
    for turn in [*range(1, chips), 0]:
        pairs += cut_pairs(k_ref, v_ref, z ^ turn, kv_refs[turn])
    for step, out in enumerate(q_refs):
        pairs.append((q_ref.at[:, cut(head ^ step, out.shape[1])], out))
    for one in copy_all(pairs, sem):
        one.wait()


def split(queries, keys, values, chips):
    rows, width = keys.shape
    groups = queries.shape[1] // width
    outs = [jax.ShapeDtypeStruct((rows, 2 * width // chips), keys.dtype)] * chips
    outs += [jax.ShapeDtypeStruct((queries.shape[0], width), queries.dtype)] * groups
    outs = pl.pallas_call(
        functools.partial(split_kernel, chips),
        out_shape=outs,
        in_specs=[HBM] * 3,
        out_specs=[ANY] * len(outs),
        scratch_shapes=[pltpu.SemaphoreType.DMA((2 * chips + groups,))],
        compiler_params=PARAMS,
    )(*(pltpu.with_memory_space_constraint(x, pltpu.HBM) for x in (queries, keys, values)))
    return outs[:chips], outs[chips:]


def regroup_kernel(chips, groups, order_ref, *rest):
    q_parts, q_refs, rel_ref = rest[:groups], rest[groups:-1], rest[-1]
    z, core, head = place()
    sub, (rows, width) = q_parts[0].shape[0], q_refs[0].shape
    for turn, out in enumerate(q_refs):
        for step, part in enumerate(q_parts):
            out[cut(head ^ step, sub), :] = part[:, cut(z ^ turn, width)]
    inner = lax.broadcasted_iota(jnp.int32, (8, rows), 1)
    starts = [
        order_ref[(z ^ (slot % chips)) * CORES + (core ^ (slot // chips))] * rows for slot in range(chips * CORES)
    ]
    for turn in range(chips):
        for slot, start in enumerate(starts):
            rel_ref[turn, :, pl.ds(slot * rows, rows)] = inner + (start - starts[turn])


def regroup(block_order, q_parts, rows, chips):
    outs = [jax.ShapeDtypeStruct((rows, q_parts[0].shape[1] // chips), q_parts[0].dtype)] * chips
    outs += [jax.ShapeDtypeStruct((chips, 8, rows * chips * CORES), jnp.int32)]
    outs = pl.pallas_call(
        functools.partial(regroup_kernel, chips, len(q_parts)),
        out_shape=outs,
        in_specs=[SMEM] + [VMEM] * len(q_parts),
        out_specs=[VMEM] * len(outs),
        compiler_params=PARAMS,
    )(block_order, *q_parts)
    return outs[:-1], outs[-1]


def stack_kernel(*refs):
    for at, ref in enumerate(refs[:-1]):
        refs[-1][at] = ref[...]


def stack(parts):
    return pl.pallas_call(
        stack_kernel,
        out_shape=jax.ShapeDtypeStruct((len(parts),) + parts[0].shape, parts[0].dtype),
        in_specs=[VMEM] * len(parts),
        out_specs=VMEM,
        compiler_params=PARAMS,
        cost_estimate=STACK_COST,
    )(*parts)


def attend_kernel(turns, count, first, last, stacked, alone, rel_ref, *rest):
    q_refs, rest = rest[: len(turns)], rest[len(turns) :]
    blocks, states, outs = [], (), ()
    if first:
        blocks, rest = list(rest[:count]), rest[count:]
    if last:
        others = {turn: rest[0].at[at] for at, turn in enumerate(stacked)} | dict(zip(alone, rest[1:]))
        blocks, rest = blocks + [others[turn] for turn in range(count)], rest[1 + len(alone) :]
        outs, rest = rest[len(rest) - len(turns) :], rest[: len(rest) - len(turns)]
    if not (first and last):
        states = rest[: 2 * len(turns)]
    rows, width = q_refs[0].shape
    scale = LOG2E / HEAD_DIM**0.5
    below = lax.broadcasted_iota(jnp.int32, (rows, CORES * rows), 0)
    ones = jnp.ones((CORES * rows, HEAD_DIM), jnp.bfloat16)
    start = 0 if first else count * rows

    def both(at, column):
        return jnp.concatenate([ref[:, pl.ds(column, HEAD_DIM)] for ref in blocks[at : at + CORES]], 0)

    for index, (turn, q_ref) in enumerate(zip(turns, q_refs)):
        top_ref, sums_ref = states[2 * index : 2 * index + 2] or (None, None)
        for column in range(0, width, HEAD_DIM):
            tops, wide = pl.ds(column, HEAD_DIM), pl.ds(2 * column, 2 * HEAD_DIM)
            top = None if first else top_ref[:, tops]
            sums = None if first else sums_ref[:, wide]
            for at in range(0, len(blocks), CORES):
                s = lax.dot_general(
                    q_ref[:, tops], both(at, column), (((1,), (1,)), ((), ())), preferred_element_type=jnp.float32
                )
                rel = rel_ref[turn, 0:1, pl.ds(start + at * rows, CORES * rows)]
                s = jnp.where(rel <= below, s, jnp.float32(-1e30))
                high = jnp.broadcast_to(jnp.max(s, axis=1, keepdims=True), (rows, HEAD_DIM))
                high = high if top is None else jnp.maximum(top, high)
                weight = jnp.exp2((s - jnp.concatenate([high] * CORES, 1)) * scale).astype(jnp.bfloat16)
                values = jnp.concatenate([both(at, width + column), ones], 1)
                mixed = jnp.dot(weight, values, preferred_element_type=jnp.float32)
                if top is not None:
                    shrink = jnp.exp2((top - high) * scale)
                    mixed += sums * jnp.concatenate([shrink, shrink], 1)
                top, sums = high, mixed
            if last:
                outs[index][:, tops] = (sums[:, :HEAD_DIM] / sums[:, HEAD_DIM:]).astype(outs[index].dtype)
            else:
                top_ref[:, tops], sums_ref[:, wide] = top, sums


def attend_near(turns, rel, q, near):
    rows, width = q[0].shape
    state = [jax.ShapeDtypeStruct((rows, wide), jnp.float32) for wide in (width, 2 * width)]
    outs = pl.pallas_call(
        functools.partial(attend_kernel, turns, len(near), True, False, (), ()),
        out_shape=state * len(turns),
        in_specs=[VMEM] * (1 + len(turns) + len(near)),
        out_specs=[VMEM] * (2 * len(turns)),
        compiler_params=PARAMS,
        cost_estimate=NEAR_COST,
    )(rel, *(q[turn] for turn in turns), *near)
    return {turn: outs[2 * index : 2 * index + 2] for index, turn in enumerate(turns)}


def attend(turns, rel, q, near, far, states, *after):
    stacked, swap, alone = far
    given = [*near, swap, *alone.values(), *(part for turn in turns for part in states.get(turn, ()))]
    outs = pl.pallas_call(
        functools.partial(attend_kernel, turns, len(q), bool(near), True, stacked, tuple(alone)),
        out_shape=[jax.ShapeDtypeStruct(q[0].shape, q[0].dtype)] * len(turns),
        in_specs=[VMEM] * (1 + len(turns) + len(given)) + [ANY] * len(after),
        out_specs=[VMEM] * len(turns),
        compiler_params=PARAMS,
    )(rel, *(q[turn] for turn in turns), *given, *after)
    return dict(zip(turns, outs))


def join_kernel(chips, *refs):
    parts, out, sem = refs[:chips], refs[-2], refs[-1]
    z, _, _ = place()
    width = parts[0].shape[1]
    pairs = [(part, out.at[:, cut(z ^ turn, width)]) for turn, part in enumerate(parts)]
    for one in copy_all(pairs, sem):
        one.wait()


def join(parts):
    chips, (rows, width) = len(parts), parts[0].shape
    return pl.pallas_call(
        functools.partial(join_kernel, chips),
        out_shape=jax.ShapeDtypeStruct((rows, width * chips), parts[0].dtype),
        in_specs=[ANY] * chips,
        out_specs=ANY,
        scratch_shapes=[pltpu.SemaphoreType.DMA((chips,))],
        compiler_params=PARAMS,
    )(*parts)


def by_heads(queries, keys, values, block_order):
    chips = lax.axis_size("seq") // CORES
    groups = lax.axis_size("head")
    half = chips // 2
    across, within = list(range(half, chips)), list(range(1, half))
    kv, q_cut = split(queries, keys, values, chips)
    near = [kv[0]] + [over(kv[turn], turn) for turn in range(1, chips)]
    q_parts = [q_cut[0]] + [swapped(q_cut[step], "head", step) for step in range(1, groups)]
    q, rel = regroup(block_order, q_parts, keys.shape[0], chips)
    q = [q[0]] + [over(q[turn], turn) for turn in range(1, chips)]
    stacked = [*across[::-1], 0]
    swap = swapped(stack([near[turn] for turn in stacked]), "seq", 1)
    far = (stacked, swap, {turn: swapped(near[turn], "seq", 1) for turn in within})
    states = attend_near([*within, 0], rel, q, near)
    done = attend(within, rel, q, (), far, states) if within else {}
    out = {turn: over(part, turn) for turn, part in done.items()}
    for turn in across[::-1]:
        out[turn] = over(attend([turn], rel, q, near, far, {}, *done.values())[turn], turn)
    out |= attend([0], rel, q, (), far, states)
    return join([out[turn] for turn in range(chips)])


def around_ring(queries, keys, values, block_order):
    seq_count = lax.axis_size("seq")
    me_index = lax.axis_index("seq")
    local_q = lax.all_to_all(queries, "head", split_axis=1, concat_axis=0, tiled=True)
    rows = local_q.shape[0]
    head_count = local_q.shape[1] // HEAD_DIM
    q_three = local_q.reshape(rows, head_count, HEAD_DIM)
    mine = block_order[me_index]
    scale = 1.0 / HEAD_DIM**0.5

    def tile(state, kv_pair, allowed):
        rowmax, total, accum = state
        key_count = kv_pair[0].shape[0]
        k_three = kv_pair[0].reshape(key_count, head_count, HEAD_DIM)
        v_three = kv_pair[1].reshape(key_count, head_count, HEAD_DIM)
        scores = (
            jnp.einsum("qhd,khd->hqk", q_three, k_three, preferred_element_type=jnp.float32) * scale
        )
        scores = jnp.where(allowed[None], scores, jnp.float32(-1e30))
        new_max = jnp.maximum(rowmax, jnp.max(scores, axis=2))
        factor = jnp.exp(rowmax - new_max)
        weight = jnp.where(allowed[None], jnp.exp(scores - new_max[:, :, None]), jnp.float32(0.0))
        total = total * factor + jnp.sum(weight, axis=2)
        mixed = jnp.einsum(
            "hqk,khd->qhd", weight.astype(jnp.bfloat16), v_three, preferred_element_type=jnp.float32
        )
        accum = accum * jnp.transpose(factor)[:, :, None] + mixed
        return (new_max, total, accum)

    def absorb(state, kv_pair, source):
        visible = block_order[source % seq_count] < mine
        allowed = jnp.broadcast_to(visible, (rows, rows))
        return tile(state, kv_pair, allowed)

    start_state = (
        jnp.full((head_count, rows), -1e30, jnp.float32),
        jnp.zeros((head_count, rows), jnp.float32),
        jnp.zeros((rows, head_count, HEAD_DIM), jnp.float32),
    )
    query_idx = lax.broadcasted_iota(jnp.int32, (rows, rows), 0)
    key_idx = lax.broadcasted_iota(jnp.int32, (rows, rows), 1)
    state = tile(start_state, (keys, values), key_idx <= query_idx)

    def both_turn(step, carry):
        ahead, behind, st = carry
        ahead = tuple(shifted(part, "seq", 1) for part in ahead)
        st = absorb(st, ahead, me_index - step + seq_count)
        behind = tuple(shifted(part, "seq", -1) for part in behind)
        st = absorb(st, behind, me_index + step)
        return (ahead, behind, st)

    ahead, behind, state = lax.fori_loop(
        1, (seq_count - 1) // 2 + 1, both_turn, ((keys, values), (keys, values), state)
    )
    if seq_count % 2 == 0:
        ahead = tuple(shifted(part, "seq", 1) for part in ahead)
        state = absorb(state, ahead, me_index - seq_count // 2 + seq_count)
    rowmax, total, accum = state
    result = accum / jnp.transpose(total)[:, :, None]
    return result.reshape(rows, head_count * HEAD_DIM).astype(jnp.bfloat16)


def body(queries, keys, values, block_order):
    seq_count, groups = lax.axis_size("seq"), lax.axis_size("head")
    chips = seq_count // CORES
    heads = keys.shape[1] // HEAD_DIM
    powers = all(n > 1 and n & (n - 1) == 0 for n in (chips, groups))
    if seq_count % CORES == 0 and powers and heads % chips == 0:
        return by_heads(queries, keys, values, block_order)
    return around_ring(queries, keys, values, block_order)


def solution(mesh):
    in_specs = (P(("seq", "head"), None), P("seq", "head"), P("seq", "head"), P())
    out_specs = P("seq", "head")
    return jax.shard_map(body, mesh=mesh, in_specs=in_specs, out_specs=out_specs, check_vma=False)
```

```python
import functools

import jax
import jax.numpy as jnp
from jax import lax
from jax.experimental import pallas as pl
from jax.experimental.pallas import tpu as pltpu
from jax.sharding import PartitionSpec as P

HEAD_DIM = 128
CORES = 2
LOG2E = 1.4426950408889634
ANY = pl.BlockSpec(memory_space=pl.ANY)
HBM = pl.BlockSpec(memory_space=pltpu.HBM)
VMEM = pl.BlockSpec(memory_space=pltpu.VMEM)
SMEM = pl.BlockSpec(memory_space=pltpu.SMEM)
PARAMS = pltpu.CompilerParams(vmem_limit_bytes=16 * 2**20)
STACK_COST = pl.CostEstimate(flops=20 * 10**9, bytes_accessed=0, transcendentals=0)
NEAR_COST = pl.CostEstimate(flops=60 * 10**9, bytes_accessed=0, transcendentals=0)


def shifted(block, axis, distance):
    devices = range(lax.axis_size(axis))
    route = [((i - distance) % len(devices), i) for i in devices]
    return lax.ppermute(block, axis, route)


def swapped(block, axis, bits):
    route = [(i, i ^ bits) for i in range(lax.axis_size(axis))]
    return lax.ppermute(block, axis, route)


def place():
    me = lax.axis_index("seq")
    return me // CORES, me % CORES, lax.axis_index("head")


def over(block, turn):
    return swapped(block, "seq", CORES * turn)


def cut(start, size):
    return pl.ds(pl.multiple_of(start * size, size), size)


def copy_all(pairs, sem):
    copies = [pltpu.make_async_copy(one, other, sem.at[i]) for i, (one, other) in enumerate(pairs)]
    for one in copies:
        one.start()
    return copies


def cut_pairs(k_ref, v_ref, chip, out):
    width = out.shape[1] // 2
    return [
        (k_ref.at[:, cut(chip, width)], out.at[:, pl.ds(0, width)]),
        (v_ref.at[:, cut(chip, width)], out.at[:, pl.ds(width, width)]),
    ]


def split_kernel(chips, q_ref, k_ref, v_ref, *rest):
    kv_refs, q_refs, sem = rest[:chips], rest[chips:-1], rest[-1]
    z, _, head = place()
    pairs = []
    for turn in [*range(1, chips), 0]:
        pairs += cut_pairs(k_ref, v_ref, z ^ turn, kv_refs[turn])
    for step, out in enumerate(q_refs):
        pairs.append((q_ref.at[:, cut(head ^ step, out.shape[1])], out))
    for one in copy_all(pairs, sem):
        one.wait()


def split(queries, keys, values, chips):
    rows, width = keys.shape
    groups = queries.shape[1] // width
    outs = [jax.ShapeDtypeStruct((rows, 2 * width // chips), keys.dtype)] * chips
    outs += [jax.ShapeDtypeStruct((queries.shape[0], width), queries.dtype)] * groups
    outs = pl.pallas_call(
        functools.partial(split_kernel, chips),
        out_shape=outs,
        in_specs=[HBM] * 3,
        out_specs=[ANY] * len(outs),
        scratch_shapes=[pltpu.SemaphoreType.DMA((2 * chips + groups,))],
        compiler_params=PARAMS,
    )(*(pltpu.with_memory_space_constraint(x, pltpu.HBM) for x in (queries, keys, values)))
    return outs[:chips], outs[chips:]


def measure_kernel(chips, rows, order_ref, *rest):
    rel_ref = rest[-1]
    z, core, _ = place()
    inner = lax.broadcasted_iota(jnp.int32, (8, rows), 1)
    starts = [
        order_ref[(z ^ (slot % chips)) * CORES + (core ^ (slot // chips))] * rows for slot in range(chips * CORES)
    ]
    for turn in range(chips):
        for slot, start in enumerate(starts):
            rel_ref[turn, :, pl.ds(slot * rows, rows)] = inner + (start - starts[turn])


def measure(block_order, rows, chips, *after):
    return pl.pallas_call(
        functools.partial(measure_kernel, chips, rows),
        out_shape=jax.ShapeDtypeStruct((chips, 8, rows * chips * CORES), jnp.int32),
        in_specs=[SMEM] + [ANY] * len(after),
        out_specs=VMEM,
        compiler_params=PARAMS,
    )(block_order, *after)


def regroup_kernel(groups, *refs):
    q_parts, q_refs = refs[:groups], refs[groups + 1 :]
    z, _, head = place()
    sub, (rows, width) = q_parts[0].shape[0], q_refs[0].shape
    for turn, out in enumerate(q_refs):
        for step, part in enumerate(q_parts):
            out[cut(head ^ step, sub), :] = part[:, cut(z ^ turn, width)]


def regroup(q_parts, rows, chips, after):
    return pl.pallas_call(
        functools.partial(regroup_kernel, len(q_parts)),
        out_shape=[jax.ShapeDtypeStruct((rows, q_parts[0].shape[1] // chips), q_parts[0].dtype)] * chips,
        in_specs=[VMEM] * len(q_parts) + [ANY],
        out_specs=[VMEM] * chips,
        compiler_params=PARAMS,
    )(*q_parts, after)


def stack_kernel(*refs):
    for at, ref in enumerate(refs[:-1]):
        refs[-1][at] = ref[...]


def stack(parts):
    return pl.pallas_call(
        stack_kernel,
        out_shape=jax.ShapeDtypeStruct((len(parts),) + parts[0].shape, parts[0].dtype),
        in_specs=[VMEM] * len(parts),
        out_specs=VMEM,
        compiler_params=PARAMS,
        cost_estimate=STACK_COST,
    )(*parts)


def attend_kernel(turns, count, first, last, stacked, alone, rel_ref, *rest):
    q_refs, rest = rest[: len(turns)], rest[len(turns) :]
    blocks, states, outs = [], (), ()
    if first:
        blocks, rest = list(rest[:count]), rest[count:]
    if last:
        others = {turn: rest[0].at[at] for at, turn in enumerate(stacked)} | dict(zip(alone, rest[1:]))
        blocks, rest = blocks + [others[turn] for turn in range(count)], rest[1 + len(alone) :]
        outs, rest = rest[len(rest) - len(turns) :], rest[: len(rest) - len(turns)]
    if not (first and last):
        states = rest[: 2 * len(turns)]
    rows, width = q_refs[0].shape
    scale = LOG2E / HEAD_DIM**0.5
    below = lax.broadcasted_iota(jnp.int32, (rows, CORES * rows), 0)
    ones = jnp.ones((CORES * rows, HEAD_DIM), jnp.bfloat16)
    start = 0 if first else count * rows

    def both(at, column):
        return jnp.concatenate([ref[:, pl.ds(column, HEAD_DIM)] for ref in blocks[at : at + CORES]], 0)

    for index, (turn, q_ref) in enumerate(zip(turns, q_refs)):
        top_ref, sums_ref = states[2 * index : 2 * index + 2] or (None, None)
        for column in range(0, width, HEAD_DIM):
            tops, wide = pl.ds(column, HEAD_DIM), pl.ds(2 * column, 2 * HEAD_DIM)
            top = None if first else top_ref[:, tops]
            sums = None if first else sums_ref[:, wide]
            for at in range(0, len(blocks), CORES):
                s = lax.dot_general(
                    q_ref[:, tops], both(at, column), (((1,), (1,)), ((), ())), preferred_element_type=jnp.float32
                )
                rel = rel_ref[turn, 0:1, pl.ds(start + at * rows, CORES * rows)]
                s = jnp.where(rel <= below, s, jnp.float32(-1e30))
                high = jnp.broadcast_to(jnp.max(s, axis=1, keepdims=True), (rows, HEAD_DIM))
                high = high if top is None else jnp.maximum(top, high)
                weight = jnp.exp2((s - jnp.concatenate([high] * CORES, 1)) * scale).astype(jnp.bfloat16)
                values = jnp.concatenate([both(at, width + column), ones], 1)
                mixed = jnp.dot(weight, values, preferred_element_type=jnp.float32)
                if top is not None:
                    shrink = jnp.exp2((top - high) * scale)
                    mixed += sums * jnp.concatenate([shrink, shrink], 1)
                top, sums = high, mixed
            if last:
                outs[index][:, tops] = (sums[:, :HEAD_DIM] / sums[:, HEAD_DIM:]).astype(outs[index].dtype)
            else:
                top_ref[:, tops], sums_ref[:, wide] = top, sums


def attend_near(turns, rel, q, near):
    rows, width = q[0].shape
    state = [jax.ShapeDtypeStruct((rows, wide), jnp.float32) for wide in (width, 2 * width)]
    outs = pl.pallas_call(
        functools.partial(attend_kernel, turns, len(near), True, False, (), ()),
        out_shape=state * len(turns),
        in_specs=[VMEM] * (1 + len(turns) + len(near)),
        out_specs=[VMEM] * (2 * len(turns)),
        compiler_params=PARAMS,
        cost_estimate=NEAR_COST,
    )(rel, *(q[turn] for turn in turns), *near)
    return {turn: outs[2 * index : 2 * index + 2] for index, turn in enumerate(turns)}


def attend(turns, rel, q, near, far, states, *after):
    stacked, swap, alone = far
    given = [*near, swap, *alone.values(), *(part for turn in turns for part in states.get(turn, ()))]
    outs = pl.pallas_call(
        functools.partial(attend_kernel, turns, len(q), bool(near), True, stacked, tuple(alone)),
        out_shape=[jax.ShapeDtypeStruct(q[0].shape, q[0].dtype)] * len(turns),
        in_specs=[VMEM] * (1 + len(turns) + len(given)) + [ANY] * len(after),
        out_specs=[VMEM] * len(turns),
        compiler_params=PARAMS,
    )(rel, *(q[turn] for turn in turns), *given, *after)
    return dict(zip(turns, outs))


def join_kernel(chips, *refs):
    parts, out, sem = refs[:chips], refs[-2], refs[-1]
    z, _, _ = place()
    width = parts[0].shape[1]
    pairs = [(part, out.at[:, cut(z ^ turn, width)]) for turn, part in enumerate(parts)]
    for one in copy_all(pairs, sem):
        one.wait()


def join(parts):
    chips, (rows, width) = len(parts), parts[0].shape
    return pl.pallas_call(
        functools.partial(join_kernel, chips),
        out_shape=jax.ShapeDtypeStruct((rows, width * chips), parts[0].dtype),
        in_specs=[ANY] * chips,
        out_specs=ANY,
        scratch_shapes=[pltpu.SemaphoreType.DMA((chips,))],
        compiler_params=PARAMS,
    )(*parts)


def by_heads(queries, keys, values, block_order):
    chips = lax.axis_size("seq") // CORES
    groups = lax.axis_size("head")
    half = chips // 2
    across, within = list(range(half, chips)), list(range(1, half))
    kv, q_cut = split(queries, keys, values, chips)
    near = [kv[0]] + [over(kv[turn], turn) for turn in range(1, chips)]
    q_parts = [q_cut[0]] + [swapped(q_cut[step], "head", step) for step in range(1, groups)]
    rel = measure(block_order, keys.shape[0], chips, q_parts[1])
    q = regroup(q_parts, keys.shape[0], chips, rel)
    q = [q[0]] + [over(q[turn], turn) for turn in range(1, chips)]
    stacked = [*across[::-1], 0]
    swap = swapped(stack([near[turn] for turn in stacked]), "seq", 1)
    far = (stacked, swap, {turn: swapped(near[turn], "seq", 1) for turn in within})
    states = attend_near([*within, 0], rel, q, near)
    done = attend(within, rel, q, (), far, states) if within else {}
    out = {turn: over(part, turn) for turn, part in done.items()}
    for turn in across[::-1]:
        out[turn] = over(attend([turn], rel, q, near, far, {}, *done.values())[turn], turn)
    out |= attend([0], rel, q, (), far, states)
    return join([out[turn] for turn in range(chips)])


def around_ring(queries, keys, values, block_order):
    seq_count = lax.axis_size("seq")
    me_index = lax.axis_index("seq")
    local_q = lax.all_to_all(queries, "head", split_axis=1, concat_axis=0, tiled=True)
    rows = local_q.shape[0]
    head_count = local_q.shape[1] // HEAD_DIM
    q_three = local_q.reshape(rows, head_count, HEAD_DIM)
    mine = block_order[me_index]
    scale = 1.0 / HEAD_DIM**0.5

    def tile(state, kv_pair, allowed):
        rowmax, total, accum = state
        key_count = kv_pair[0].shape[0]
        k_three = kv_pair[0].reshape(key_count, head_count, HEAD_DIM)
        v_three = kv_pair[1].reshape(key_count, head_count, HEAD_DIM)
        scores = (
            jnp.einsum("qhd,khd->hqk", q_three, k_three, preferred_element_type=jnp.float32) * scale
        )
        scores = jnp.where(allowed[None], scores, jnp.float32(-1e30))
        new_max = jnp.maximum(rowmax, jnp.max(scores, axis=2))
        factor = jnp.exp(rowmax - new_max)
        weight = jnp.where(allowed[None], jnp.exp(scores - new_max[:, :, None]), jnp.float32(0.0))
        total = total * factor + jnp.sum(weight, axis=2)
        mixed = jnp.einsum(
            "hqk,khd->qhd", weight.astype(jnp.bfloat16), v_three, preferred_element_type=jnp.float32
        )
        accum = accum * jnp.transpose(factor)[:, :, None] + mixed
        return (new_max, total, accum)

    def absorb(state, kv_pair, source):
        visible = block_order[source % seq_count] < mine
        allowed = jnp.broadcast_to(visible, (rows, rows))
        return tile(state, kv_pair, allowed)

    start_state = (
        jnp.full((head_count, rows), -1e30, jnp.float32),
        jnp.zeros((head_count, rows), jnp.float32),
        jnp.zeros((rows, head_count, HEAD_DIM), jnp.float32),
    )
    query_idx = lax.broadcasted_iota(jnp.int32, (rows, rows), 0)
    key_idx = lax.broadcasted_iota(jnp.int32, (rows, rows), 1)
    state = tile(start_state, (keys, values), key_idx <= query_idx)

    def both_turn(step, carry):
        ahead, behind, st = carry
        ahead = tuple(shifted(part, "seq", 1) for part in ahead)
        st = absorb(st, ahead, me_index - step + seq_count)
        behind = tuple(shifted(part, "seq", -1) for part in behind)
        st = absorb(st, behind, me_index + step)
        return (ahead, behind, st)

    ahead, behind, state = lax.fori_loop(
        1, (seq_count - 1) // 2 + 1, both_turn, ((keys, values), (keys, values), state)
    )
    if seq_count % 2 == 0:
        ahead = tuple(shifted(part, "seq", 1) for part in ahead)
        state = absorb(state, ahead, me_index - seq_count // 2 + seq_count)
    rowmax, total, accum = state
    result = accum / jnp.transpose(total)[:, :, None]
    return result.reshape(rows, head_count * HEAD_DIM).astype(jnp.bfloat16)


def body(queries, keys, values, block_order):
    seq_count, groups = lax.axis_size("seq"), lax.axis_size("head")
    chips = seq_count // CORES
    heads = keys.shape[1] // HEAD_DIM
    powers = all(n > 1 and n & (n - 1) == 0 for n in (chips, groups))
    if seq_count % CORES == 0 and powers and heads % chips == 0:
        return by_heads(queries, keys, values, block_order)
    return around_ring(queries, keys, values, block_order)


def solution(mesh):
    in_specs = (P(("seq", "head"), None), P("seq", "head"), P("seq", "head"), P())
    out_specs = P("seq", "head")
    return jax.shard_map(body, mesh=mesh, in_specs=in_specs, out_specs=out_specs, check_vma=False)
```

```python
import functools

import jax
import jax.numpy as jnp
from jax import lax
from jax.experimental import pallas as pl
from jax.experimental.pallas import tpu as pltpu
from jax.sharding import PartitionSpec as P

HEAD_DIM = 128
CORES = 2
LOG2E = 1.4426950408889634
ANY = pl.BlockSpec(memory_space=pl.ANY)
HBM = pl.BlockSpec(memory_space=pltpu.HBM)
VMEM = pl.BlockSpec(memory_space=pltpu.VMEM)
SMEM = pl.BlockSpec(memory_space=pltpu.SMEM)
PARAMS = pltpu.CompilerParams(vmem_limit_bytes=16 * 2**20)
STACK_COST = pl.CostEstimate(flops=20 * 10**9, bytes_accessed=0, transcendentals=0)
NEAR_COST = pl.CostEstimate(flops=60 * 10**9, bytes_accessed=0, transcendentals=0)


def shifted(block, axis, distance):
    devices = range(lax.axis_size(axis))
    route = [((i - distance) % len(devices), i) for i in devices]
    return lax.ppermute(block, axis, route)


def swapped(block, axis, bits):
    route = [(i, i ^ bits) for i in range(lax.axis_size(axis))]
    return lax.ppermute(block, axis, route)


def place():
    me = lax.axis_index("seq")
    return me // CORES, me % CORES, lax.axis_index("head")


def over(block, turn):
    return swapped(block, "seq", CORES * turn)


def cut(start, size):
    return pl.ds(pl.multiple_of(start * size, size), size)


def copy_all(pairs, sem):
    copies = [pltpu.make_async_copy(one, other, sem.at[i]) for i, (one, other) in enumerate(pairs)]
    for one in copies:
        one.start()
    return copies


def cut_pairs(k_ref, v_ref, chip, out):
    width = out.shape[1] // 2
    return [
        (k_ref.at[:, cut(chip, width)], out.at[:, pl.ds(0, width)]),
        (v_ref.at[:, cut(chip, width)], out.at[:, pl.ds(width, width)]),
    ]


def split_kernel(turns, q_ref, k_ref, v_ref, *rest):
    kv_refs, q_refs, sem = rest[: len(turns)], rest[len(turns) : -1], rest[-1]
    z, _, head = place()
    pairs = []
    for turn, out in zip(turns, kv_refs):
        pairs += cut_pairs(k_ref, v_ref, z ^ turn, out)
    for step, out in enumerate(q_refs, 1):
        pairs.append((q_ref.at[:, cut(head ^ step, out.shape[1])], out))
    for one in copy_all(pairs, sem):
        one.wait()


def split(queries, keys, values, turns, chips):
    rows, width = keys.shape
    others = queries.shape[1] // width - 1
    outs = [jax.ShapeDtypeStruct((rows, 2 * width // chips), keys.dtype)] * len(turns)
    outs += [jax.ShapeDtypeStruct((queries.shape[0], width), queries.dtype)] * others
    outs = pl.pallas_call(
        functools.partial(split_kernel, turns),
        out_shape=outs,
        in_specs=[HBM] * 3,
        out_specs=[ANY] * len(outs),
        scratch_shapes=[pltpu.SemaphoreType.DMA((2 * len(turns) + others,))],
        compiler_params=PARAMS,
    )(*in_hbm(queries, keys, values))
    return dict(zip(turns, outs)), outs[len(turns) :]


def in_hbm(*arrays):
    return [pltpu.with_memory_space_constraint(x, pltpu.HBM) for x in arrays]


def measure_kernel(turns, chips, order_ref, q_ref, k_ref, v_ref, _, *rest):
    kv_refs, q_out, rel_ref, sem = rest[: len(turns)], rest[-3], rest[-2], rest[-1]
    z, core, head = place()
    rows = k_ref.shape[0]
    pairs = [(q_ref.at[:, cut(head, q_out.shape[1])], q_out)]
    for turn, out in zip(turns, kv_refs):
        pairs += cut_pairs(k_ref, v_ref, z ^ turn, out)
    copies = copy_all(pairs, sem)
    inner = lax.broadcasted_iota(jnp.int32, (8, rows), 1)
    starts = [
        order_ref[(z ^ (slot % chips)) * CORES + (core ^ (slot // chips))] * rows for slot in range(chips * CORES)
    ]
    for turn in range(chips):
        for slot, start in enumerate(starts):
            rel_ref[turn, :, pl.ds(slot * rows, rows)] = inner + (start - starts[turn])
    for one in copies:
        one.wait()


def measure(block_order, queries, keys, values, turns, chips, after):
    rows, width = keys.shape
    outs = [jax.ShapeDtypeStruct((rows, 2 * width // chips), keys.dtype)] * len(turns)
    outs += [
        jax.ShapeDtypeStruct((queries.shape[0], width), queries.dtype),
        jax.ShapeDtypeStruct((chips, 8, rows * chips * CORES), jnp.int32),
    ]
    outs = pl.pallas_call(
        functools.partial(measure_kernel, turns, chips),
        out_shape=outs,
        in_specs=[SMEM] + [HBM] * 3 + [ANY],
        out_specs=[ANY] * (len(turns) + 1) + [VMEM],
        scratch_shapes=[pltpu.SemaphoreType.DMA((2 * len(turns) + 1,))],
        compiler_params=PARAMS,
    )(block_order, *in_hbm(queries, keys, values), after)
    return dict(zip(turns, outs)), outs[-2], outs[-1]


def regroup_kernel(groups, *refs):
    q_parts, q_refs = refs[:groups], refs[groups + 1 :]
    z, _, head = place()
    sub, (rows, width) = q_parts[0].shape[0], q_refs[0].shape
    for turn, out in enumerate(q_refs):
        for step, part in enumerate(q_parts):
            out[cut(head ^ step, sub), :] = part[:, cut(z ^ turn, width)]


def regroup(q_parts, rows, chips, after):
    return pl.pallas_call(
        functools.partial(regroup_kernel, len(q_parts)),
        out_shape=[jax.ShapeDtypeStruct((rows, q_parts[0].shape[1] // chips), q_parts[0].dtype)] * chips,
        in_specs=[VMEM] * len(q_parts) + [ANY],
        out_specs=[VMEM] * chips,
        compiler_params=PARAMS,
    )(*q_parts, after)


def stack_kernel(*refs):
    for at, ref in enumerate(refs[:-1]):
        refs[-1][at] = ref[...]


def stack(parts):
    return pl.pallas_call(
        stack_kernel,
        out_shape=jax.ShapeDtypeStruct((len(parts),) + parts[0].shape, parts[0].dtype),
        in_specs=[VMEM] * len(parts),
        out_specs=VMEM,
        compiler_params=PARAMS,
        cost_estimate=STACK_COST,
    )(*parts)


def attend_kernel(turns, count, first, last, stacked, alone, rel_ref, *rest):
    q_refs, rest = rest[: len(turns)], rest[len(turns) :]
    blocks, states, outs = [], (), ()
    if first:
        blocks, rest = list(rest[:count]), rest[count:]
    if last:
        others = {turn: rest[0].at[at] for at, turn in enumerate(stacked)} | dict(zip(alone, rest[1:]))
        blocks, rest = blocks + [others[turn] for turn in range(count)], rest[1 + len(alone) :]
        outs, rest = rest[len(rest) - len(turns) :], rest[: len(rest) - len(turns)]
    if not (first and last):
        states = rest[: 2 * len(turns)]
    rows, width = q_refs[0].shape
    scale = LOG2E / HEAD_DIM**0.5
    below = lax.broadcasted_iota(jnp.int32, (rows, CORES * rows), 0)
    ones = jnp.ones((CORES * rows, HEAD_DIM), jnp.bfloat16)
    start = 0 if first else count * rows

    def both(at, column):
        return jnp.concatenate([ref[:, pl.ds(column, HEAD_DIM)] for ref in blocks[at : at + CORES]], 0)

    for index, (turn, q_ref) in enumerate(zip(turns, q_refs)):
        top_ref, sums_ref = states[2 * index : 2 * index + 2] or (None, None)
        for column in range(0, width, HEAD_DIM):
            tops, wide = pl.ds(column, HEAD_DIM), pl.ds(2 * column, 2 * HEAD_DIM)
            top = None if first else top_ref[:, tops]
            sums = None if first else sums_ref[:, wide]
            for at in range(0, len(blocks), CORES):
                s = lax.dot_general(
                    q_ref[:, tops], both(at, column), (((1,), (1,)), ((), ())), preferred_element_type=jnp.float32
                )
                rel = rel_ref[turn, 0:1, pl.ds(start + at * rows, CORES * rows)]
                s = jnp.where(rel <= below, s, jnp.float32(-1e30))
                high = jnp.broadcast_to(jnp.max(s, axis=1, keepdims=True), (rows, HEAD_DIM))
                high = high if top is None else jnp.maximum(top, high)
                weight = jnp.exp2((s - jnp.concatenate([high] * CORES, 1)) * scale).astype(jnp.bfloat16)
                values = jnp.concatenate([both(at, width + column), ones], 1)
                mixed = jnp.dot(weight, values, preferred_element_type=jnp.float32)
                if top is not None:
                    shrink = jnp.exp2((top - high) * scale)
                    mixed += sums * jnp.concatenate([shrink, shrink], 1)
                top, sums = high, mixed
            if last:
                outs[index][:, tops] = (sums[:, :HEAD_DIM] / sums[:, HEAD_DIM:]).astype(outs[index].dtype)
            else:
                top_ref[:, tops], sums_ref[:, wide] = top, sums


def attend_near(turns, rel, q, near):
    rows, width = q[0].shape
    state = [jax.ShapeDtypeStruct((rows, wide), jnp.float32) for wide in (width, 2 * width)]
    outs = pl.pallas_call(
        functools.partial(attend_kernel, turns, len(near), True, False, (), ()),
        out_shape=state * len(turns),
        in_specs=[VMEM] * (1 + len(turns) + len(near)),
        out_specs=[VMEM] * (2 * len(turns)),
        compiler_params=PARAMS,
        cost_estimate=NEAR_COST,
    )(rel, *(q[turn] for turn in turns), *near)
    return {turn: outs[2 * index : 2 * index + 2] for index, turn in enumerate(turns)}


def attend(turns, rel, q, near, far, states, *after):
    stacked, swap, alone = far
    given = [*near, swap, *alone.values(), *(part for turn in turns for part in states.get(turn, ()))]
    outs = pl.pallas_call(
        functools.partial(attend_kernel, turns, len(q), bool(near), True, stacked, tuple(alone)),
        out_shape=[jax.ShapeDtypeStruct(q[0].shape, q[0].dtype)] * len(turns),
        in_specs=[VMEM] * (1 + len(turns) + len(given)) + [ANY] * len(after),
        out_specs=[VMEM] * len(turns),
        compiler_params=PARAMS,
    )(rel, *(q[turn] for turn in turns), *given, *after)
    return dict(zip(turns, outs))


def join_kernel(chips, *refs):
    parts, out = refs[:chips], refs[-1]
    z, _, _ = place()
    width = parts[0].shape[1]
    for turn, part in enumerate(parts):
        out[:, cut(z ^ turn, width)] = part[...]


def join(parts):
    chips, (rows, width) = len(parts), parts[0].shape
    return pl.pallas_call(
        functools.partial(join_kernel, chips),
        out_shape=jax.ShapeDtypeStruct((rows, width * chips), parts[0].dtype),
        in_specs=[VMEM] * chips,
        out_specs=VMEM,
        compiler_params=PARAMS,
    )(*parts)


def by_heads(queries, keys, values, block_order):
    chips = lax.axis_size("seq") // CORES
    groups = lax.axis_size("head")
    half = chips // 2
    across, within = list(range(half, chips)), list(range(1, half))
    kv, q_cut = split(queries, keys, values, [*across[::-1], *within], chips)
    q_parts = [swapped(part, "head", step) for step, part in enumerate(q_cut, 1)]
    kv_late, q_own, rel = measure(block_order, queries, keys, values, [0], chips, q_parts[0])
    kv |= kv_late
    near = [kv[0]] + [over(kv[turn], turn) for turn in range(1, chips)]
    q = regroup([q_own, *q_parts], keys.shape[0], chips, rel)
    q = [q[0]] + [over(q[turn], turn) for turn in range(1, chips)]
    stacked = [*across[::-1], 0]
    swap = swapped(stack([near[turn] for turn in stacked]), "seq", 1)
    far = (stacked, swap, {turn: swapped(near[turn], "seq", 1) for turn in within})
    states = attend_near([*within, 0], rel, q, near)
    done = attend(within, rel, q, (), far, states) if within else {}
    out = {turn: over(part, turn) for turn, part in done.items()}
    for turn in across[::-1]:
        out[turn] = over(attend([turn], rel, q, near, far, {}, *done.values())[turn], turn)
    out |= attend([0], rel, q, (), far, states)
    return join([out[turn] for turn in range(chips)])


def around_ring(queries, keys, values, block_order):
    seq_count = lax.axis_size("seq")
    me_index = lax.axis_index("seq")
    local_q = lax.all_to_all(queries, "head", split_axis=1, concat_axis=0, tiled=True)
    rows = local_q.shape[0]
    head_count = local_q.shape[1] // HEAD_DIM
    q_three = local_q.reshape(rows, head_count, HEAD_DIM)
    mine = block_order[me_index]
    scale = 1.0 / HEAD_DIM**0.5

    def tile(state, kv_pair, allowed):
        rowmax, total, accum = state
        key_count = kv_pair[0].shape[0]
        k_three = kv_pair[0].reshape(key_count, head_count, HEAD_DIM)
        v_three = kv_pair[1].reshape(key_count, head_count, HEAD_DIM)
        scores = (
            jnp.einsum("qhd,khd->hqk", q_three, k_three, preferred_element_type=jnp.float32) * scale
        )
        scores = jnp.where(allowed[None], scores, jnp.float32(-1e30))
        new_max = jnp.maximum(rowmax, jnp.max(scores, axis=2))
        factor = jnp.exp(rowmax - new_max)
        weight = jnp.where(allowed[None], jnp.exp(scores - new_max[:, :, None]), jnp.float32(0.0))
        total = total * factor + jnp.sum(weight, axis=2)
        mixed = jnp.einsum(
            "hqk,khd->qhd", weight.astype(jnp.bfloat16), v_three, preferred_element_type=jnp.float32
        )
        accum = accum * jnp.transpose(factor)[:, :, None] + mixed
        return (new_max, total, accum)

    def absorb(state, kv_pair, source):
        visible = block_order[source % seq_count] < mine
        allowed = jnp.broadcast_to(visible, (rows, rows))
        return tile(state, kv_pair, allowed)

    start_state = (
        jnp.full((head_count, rows), -1e30, jnp.float32),
        jnp.zeros((head_count, rows), jnp.float32),
        jnp.zeros((rows, head_count, HEAD_DIM), jnp.float32),
    )
    query_idx = lax.broadcasted_iota(jnp.int32, (rows, rows), 0)
    key_idx = lax.broadcasted_iota(jnp.int32, (rows, rows), 1)
    state = tile(start_state, (keys, values), key_idx <= query_idx)

    def both_turn(step, carry):
        ahead, behind, st = carry
        ahead = tuple(shifted(part, "seq", 1) for part in ahead)
        st = absorb(st, ahead, me_index - step + seq_count)
        behind = tuple(shifted(part, "seq", -1) for part in behind)
        st = absorb(st, behind, me_index + step)
        return (ahead, behind, st)

    ahead, behind, state = lax.fori_loop(
        1, (seq_count - 1) // 2 + 1, both_turn, ((keys, values), (keys, values), state)
    )
    if seq_count % 2 == 0:
        ahead = tuple(shifted(part, "seq", 1) for part in ahead)
        state = absorb(state, ahead, me_index - seq_count // 2 + seq_count)
    rowmax, total, accum = state
    result = accum / jnp.transpose(total)[:, :, None]
    return result.reshape(rows, head_count * HEAD_DIM).astype(jnp.bfloat16)


def body(queries, keys, values, block_order):
    seq_count, groups = lax.axis_size("seq"), lax.axis_size("head")
    chips = seq_count // CORES
    heads = keys.shape[1] // HEAD_DIM
    powers = all(n > 1 and n & (n - 1) == 0 for n in (chips, groups))
    if seq_count % CORES == 0 and powers and heads % chips == 0:
        return by_heads(queries, keys, values, block_order)
    return around_ring(queries, keys, values, block_order)


def solution(mesh):
    in_specs = (P(("seq", "head"), None), P("seq", "head"), P("seq", "head"), P())
    out_specs = P("seq", "head")
    return jax.shard_map(body, mesh=mesh, in_specs=in_specs, out_specs=out_specs, check_vma=False)
```

```python
import functools

import jax
import jax.numpy as jnp
from jax import lax
from jax.experimental import pallas as pl
from jax.experimental.pallas import tpu as pltpu
from jax.sharding import PartitionSpec as P

HEAD_DIM = 128
CORES = 2
LOG2E = 1.4426950408889634
ANY = pl.BlockSpec(memory_space=pl.ANY)
HBM = pl.BlockSpec(memory_space=pltpu.HBM)
VMEM = pl.BlockSpec(memory_space=pltpu.VMEM)
SMEM = pl.BlockSpec(memory_space=pltpu.SMEM)
PARAMS = pltpu.CompilerParams(vmem_limit_bytes=16 * 2**20)
STACK_COST = pl.CostEstimate(flops=20 * 10**9, bytes_accessed=0, transcendentals=0)
NEAR_COST = pl.CostEstimate(flops=60 * 10**9, bytes_accessed=0, transcendentals=0)


def shifted(block, axis, distance):
    devices = range(lax.axis_size(axis))
    route = [((i - distance) % len(devices), i) for i in devices]
    return lax.ppermute(block, axis, route)


def swapped(block, axis, bits):
    route = [(i, i ^ bits) for i in range(lax.axis_size(axis))]
    return lax.ppermute(block, axis, route)


def place():
    me = lax.axis_index("seq")
    return me // CORES, me % CORES, lax.axis_index("head")


def over(block, turn):
    return swapped(block, "seq", CORES * turn)


def cut(start, size):
    return pl.ds(pl.multiple_of(start * size, size), size)


def copy_all(pairs, sem):
    copies = [pltpu.make_async_copy(one, other, sem.at[i]) for i, (one, other) in enumerate(pairs)]
    for one in copies:
        one.start()
    return copies


def cut_pairs(k_ref, v_ref, chip, out):
    width = out.shape[1] // 2
    return [
        (k_ref.at[:, cut(chip, width)], out.at[:, pl.ds(0, width)]),
        (v_ref.at[:, cut(chip, width)], out.at[:, pl.ds(width, width)]),
    ]


def split_kernel(turns, q_ref, k_ref, v_ref, *rest):
    kv_refs, q_refs, sem = rest[: len(turns)], rest[len(turns) : -1], rest[-1]
    z, _, head = place()
    pairs = []
    for turn, out in zip(turns, kv_refs):
        pairs += cut_pairs(k_ref, v_ref, z ^ turn, out)
    for step, out in enumerate(q_refs, 1):
        pairs.append((q_ref.at[:, cut(head ^ step, out.shape[1])], out))
    for one in copy_all(pairs, sem):
        one.wait()


def split(queries, keys, values, turns, chips):
    rows, width = keys.shape
    others = queries.shape[1] // width - 1
    outs = [jax.ShapeDtypeStruct((rows, 2 * width // chips), keys.dtype)] * len(turns)
    outs += [jax.ShapeDtypeStruct((queries.shape[0], width), queries.dtype)] * others
    outs = pl.pallas_call(
        functools.partial(split_kernel, turns),
        out_shape=outs,
        in_specs=[HBM] * 3,
        out_specs=[ANY] * len(outs),
        scratch_shapes=[pltpu.SemaphoreType.DMA((2 * len(turns) + others,))],
        compiler_params=PARAMS,
    )(*in_hbm(queries, keys, values))
    return dict(zip(turns, outs)), outs[len(turns) :]


def in_hbm(*arrays):
    return [pltpu.with_memory_space_constraint(x, pltpu.HBM) for x in arrays]


def measure_kernel(turns, chips, order_ref, q_ref, k_ref, v_ref, _, *rest):
    kv_refs, q_out, rel_ref, sem = rest[: len(turns)], rest[-3], rest[-2], rest[-1]
    z, core, head = place()
    rows = k_ref.shape[0]
    pairs = [(q_ref.at[:, cut(head, q_out.shape[1])], q_out)]
    for turn, out in zip(turns, kv_refs):
        pairs += cut_pairs(k_ref, v_ref, z ^ turn, out)
    copies = copy_all(pairs, sem)
    inner = lax.broadcasted_iota(jnp.int32, (8, rows), 1)
    starts = [
        order_ref[(z ^ (slot % chips)) * CORES + (core ^ (slot // chips))] * rows for slot in range(chips * CORES)
    ]
    for turn in range(chips):
        for slot, start in enumerate(starts):
            rel_ref[turn, :, pl.ds(slot * rows, rows)] = inner + (start - starts[turn])
    for one in copies:
        one.wait()


def measure(block_order, queries, keys, values, turns, chips, after):
    rows, width = keys.shape
    outs = [jax.ShapeDtypeStruct((rows, 2 * width // chips), keys.dtype)] * len(turns)
    outs += [
        jax.ShapeDtypeStruct((queries.shape[0], width), queries.dtype),
        jax.ShapeDtypeStruct((chips, 8, rows * chips * CORES), jnp.int32),
    ]
    outs = pl.pallas_call(
        functools.partial(measure_kernel, turns, chips),
        out_shape=outs,
        in_specs=[SMEM] + [HBM] * 3 + [ANY],
        out_specs=[ANY] * (len(turns) + 1) + [VMEM],
        scratch_shapes=[pltpu.SemaphoreType.DMA((2 * len(turns) + 1,))],
        compiler_params=PARAMS,
    )(block_order, *in_hbm(queries, keys, values), after)
    return dict(zip(turns, outs)), outs[-2], outs[-1]


def regroup_kernel(groups, *refs):
    q_parts, q_refs = refs[:groups], refs[groups + 1 :]
    z, _, head = place()
    sub, (rows, width) = q_parts[0].shape[0], q_refs[0].shape
    for turn, out in enumerate(q_refs):
        for step, part in enumerate(q_parts):
            out[cut(head ^ step, sub), :] = part[:, cut(z ^ turn, width)]


def regroup(q_parts, rows, chips, after):
    return pl.pallas_call(
        functools.partial(regroup_kernel, len(q_parts)),
        out_shape=[jax.ShapeDtypeStruct((rows, q_parts[0].shape[1] // chips), q_parts[0].dtype)] * chips,
        in_specs=[VMEM] * len(q_parts) + [ANY],
        out_specs=[VMEM] * chips,
        compiler_params=PARAMS,
    )(*q_parts, after)


def stack_kernel(*refs):
    for at, ref in enumerate(refs[:-1]):
        refs[-1][at] = ref[...]


def stack(parts):
    return pl.pallas_call(
        stack_kernel,
        out_shape=jax.ShapeDtypeStruct((len(parts),) + parts[0].shape, parts[0].dtype),
        in_specs=[VMEM] * len(parts),
        out_specs=VMEM,
        compiler_params=PARAMS,
        cost_estimate=STACK_COST,
    )(*parts)


def attend_kernel(turns, count, first, last, stacked, alone, rel_ref, *rest):
    q_refs, rest = rest[: len(turns)], rest[len(turns) :]
    blocks, states, outs = [], (), ()
    if first:
        blocks, rest = list(rest[:count]), rest[count:]
    if last:
        others = {turn: rest[0].at[at] for at, turn in enumerate(stacked)} | dict(zip(alone, rest[1:]))
        blocks, rest = blocks + [others[turn] for turn in range(count)], rest[1 + len(alone) :]
        outs, rest = rest[len(rest) - len(turns) :], rest[: len(rest) - len(turns)]
    if not (first and last):
        states = rest[: 2 * len(turns)]
    rows, width = q_refs[0].shape
    scale = LOG2E / HEAD_DIM**0.5
    below = lax.broadcasted_iota(jnp.int32, (rows, CORES * rows), 0)
    ones = jnp.ones((CORES * rows, HEAD_DIM), jnp.bfloat16)
    start = 0 if first else count * rows

    def both(at, column):
        return jnp.concatenate([ref[:, pl.ds(column, HEAD_DIM)] for ref in blocks[at : at + CORES]], 0)

    for index, (turn, q_ref) in enumerate(zip(turns, q_refs)):
        top_ref, sums_ref = states[2 * index : 2 * index + 2] or (None, None)
        columns = range(0, width, HEAD_DIM)
        state = {column: None if first else (top_ref[:, pl.ds(column, HEAD_DIM)], sums_ref[:, pl.ds(2 * column, 2 * HEAD_DIM)]) for column in columns}
        for at in range(0, len(blocks), CORES):
            seen = rel_ref[turn, 0:1, pl.ds(start + at * rows, CORES * rows)] <= below
            for column in columns:
                s = lax.dot_general(
                    q_ref[:, pl.ds(column, HEAD_DIM)],
                    both(at, column),
                    (((1,), (1,)), ((), ())),
                    preferred_element_type=jnp.float32,
                )
                s = jnp.where(seen, s, jnp.float32(-1e30))
                high = jnp.broadcast_to(jnp.max(s, axis=1, keepdims=True), (rows, HEAD_DIM))
                if state[column] is not None:
                    top, sums = state[column]
                    high = jnp.maximum(top, high)
                weight = jnp.exp2((s - jnp.concatenate([high] * CORES, 1)) * scale).astype(jnp.bfloat16)
                values = jnp.concatenate([both(at, width + column), ones], 1)
                mixed = jnp.dot(weight, values, preferred_element_type=jnp.float32)
                if state[column] is not None:
                    shrink = jnp.exp2((top - high) * scale)
                    mixed += sums * jnp.concatenate([shrink, shrink], 1)
                state[column] = (high, mixed)
        for column, (top, sums) in state.items():
            if last:
                mean = sums[:, :HEAD_DIM] / sums[:, HEAD_DIM:]
                outs[index][:, pl.ds(column, HEAD_DIM)] = mean.astype(outs[index].dtype)
            else:
                top_ref[:, pl.ds(column, HEAD_DIM)] = top
                sums_ref[:, pl.ds(2 * column, 2 * HEAD_DIM)] = sums


def attend_near(turns, rel, q, near):
    rows, width = q[0].shape
    state = [jax.ShapeDtypeStruct((rows, wide), jnp.float32) for wide in (width, 2 * width)]
    outs = pl.pallas_call(
        functools.partial(attend_kernel, turns, len(near), True, False, (), ()),
        out_shape=state * len(turns),
        in_specs=[VMEM] * (1 + len(turns) + len(near)),
        out_specs=[VMEM] * (2 * len(turns)),
        compiler_params=PARAMS,
        cost_estimate=NEAR_COST,
    )(rel, *(q[turn] for turn in turns), *near)
    return {turn: outs[2 * index : 2 * index + 2] for index, turn in enumerate(turns)}


def attend(turns, rel, q, near, far, states, *after):
    stacked, swap, alone = far
    given = [*near, swap, *alone.values(), *(part for turn in turns for part in states.get(turn, ()))]
    outs = pl.pallas_call(
        functools.partial(attend_kernel, turns, len(q), bool(near), True, stacked, tuple(alone)),
        out_shape=[jax.ShapeDtypeStruct(q[0].shape, q[0].dtype)] * len(turns),
        in_specs=[VMEM] * (1 + len(turns) + len(given)) + [ANY] * len(after),
        out_specs=[VMEM] * len(turns),
        compiler_params=PARAMS,
    )(rel, *(q[turn] for turn in turns), *given, *after)
    return dict(zip(turns, outs))


def join_kernel(chips, *refs):
    parts, out = refs[:chips], refs[-1]
    z, _, _ = place()
    width = parts[0].shape[1]
    for turn, part in enumerate(parts):
        out[:, cut(z ^ turn, width)] = part[...]


def join(parts):
    chips, (rows, width) = len(parts), parts[0].shape
    return pl.pallas_call(
        functools.partial(join_kernel, chips),
        out_shape=jax.ShapeDtypeStruct((rows, width * chips), parts[0].dtype),
        in_specs=[VMEM] * chips,
        out_specs=VMEM,
        compiler_params=PARAMS,
    )(*parts)


def by_heads(queries, keys, values, block_order):
    chips = lax.axis_size("seq") // CORES
    groups = lax.axis_size("head")
    half = chips // 2
    across, within = list(range(half, chips)), list(range(1, half))
    kv, q_cut = split(queries, keys, values, [*across[::-1], *within], chips)
    q_parts = [swapped(part, "head", step) for step, part in enumerate(q_cut, 1)]
    kv_late, q_own, rel = measure(block_order, queries, keys, values, [0], chips, q_parts[0])
    kv |= kv_late
    near = [kv[0]] + [over(kv[turn], turn) for turn in range(1, chips)]
    q = regroup([q_own, *q_parts], keys.shape[0], chips, rel)
    q = [q[0]] + [over(q[turn], turn) for turn in range(1, chips)]
    stacked = [*across[::-1], 0]
    swap = swapped(stack([near[turn] for turn in stacked]), "seq", 1)
    far = (stacked, swap, {turn: swapped(near[turn], "seq", 1) for turn in within})
    states = attend_near([0, *within], rel, q, near)
    done = attend(within, rel, q, (), far, states) if within else {}
    out = {turn: over(part, turn) for turn, part in done.items()}
    for turn in across[::-1]:
        out[turn] = over(attend([turn], rel, q, near, far, {}, *done.values())[turn], turn)
    out |= attend([0], rel, q, (), far, states)
    return join([out[turn] for turn in range(chips)])


def around_ring(queries, keys, values, block_order):
    seq_count = lax.axis_size("seq")
    me_index = lax.axis_index("seq")
    local_q = lax.all_to_all(queries, "head", split_axis=1, concat_axis=0, tiled=True)
    rows = local_q.shape[0]
    head_count = local_q.shape[1] // HEAD_DIM
    q_three = local_q.reshape(rows, head_count, HEAD_DIM)
    mine = block_order[me_index]
    scale = 1.0 / HEAD_DIM**0.5

    def tile(state, kv_pair, allowed):
        rowmax, total, accum = state
        key_count = kv_pair[0].shape[0]
        k_three = kv_pair[0].reshape(key_count, head_count, HEAD_DIM)
        v_three = kv_pair[1].reshape(key_count, head_count, HEAD_DIM)
        scores = (
            jnp.einsum("qhd,khd->hqk", q_three, k_three, preferred_element_type=jnp.float32) * scale
        )
        scores = jnp.where(allowed[None], scores, jnp.float32(-1e30))
        new_max = jnp.maximum(rowmax, jnp.max(scores, axis=2))
        factor = jnp.exp(rowmax - new_max)
        weight = jnp.where(allowed[None], jnp.exp(scores - new_max[:, :, None]), jnp.float32(0.0))
        total = total * factor + jnp.sum(weight, axis=2)
        mixed = jnp.einsum(
            "hqk,khd->qhd", weight.astype(jnp.bfloat16), v_three, preferred_element_type=jnp.float32
        )
        accum = accum * jnp.transpose(factor)[:, :, None] + mixed
        return (new_max, total, accum)

    def absorb(state, kv_pair, source):
        visible = block_order[source % seq_count] < mine
        allowed = jnp.broadcast_to(visible, (rows, rows))
        return tile(state, kv_pair, allowed)

    start_state = (
        jnp.full((head_count, rows), -1e30, jnp.float32),
        jnp.zeros((head_count, rows), jnp.float32),
        jnp.zeros((rows, head_count, HEAD_DIM), jnp.float32),
    )
    query_idx = lax.broadcasted_iota(jnp.int32, (rows, rows), 0)
    key_idx = lax.broadcasted_iota(jnp.int32, (rows, rows), 1)
    state = tile(start_state, (keys, values), key_idx <= query_idx)

    def both_turn(step, carry):
        ahead, behind, st = carry
        ahead = tuple(shifted(part, "seq", 1) for part in ahead)
        st = absorb(st, ahead, me_index - step + seq_count)
        behind = tuple(shifted(part, "seq", -1) for part in behind)
        st = absorb(st, behind, me_index + step)
        return (ahead, behind, st)

    ahead, behind, state = lax.fori_loop(
        1, (seq_count - 1) // 2 + 1, both_turn, ((keys, values), (keys, values), state)
    )
    if seq_count % 2 == 0:
        ahead = tuple(shifted(part, "seq", 1) for part in ahead)
        state = absorb(state, ahead, me_index - seq_count // 2 + seq_count)
    rowmax, total, accum = state
    result = accum / jnp.transpose(total)[:, :, None]
    return result.reshape(rows, head_count * HEAD_DIM).astype(jnp.bfloat16)


def body(queries, keys, values, block_order):
    seq_count, groups = lax.axis_size("seq"), lax.axis_size("head")
    chips = seq_count // CORES
    heads = keys.shape[1] // HEAD_DIM
    powers = all(n > 1 and n & (n - 1) == 0 for n in (chips, groups))
    if seq_count % CORES == 0 and powers and heads % chips == 0:
        return by_heads(queries, keys, values, block_order)
    return around_ring(queries, keys, values, block_order)


def solution(mesh):
    in_specs = (P(("seq", "head"), None), P("seq", "head"), P("seq", "head"), P())
    out_specs = P("seq", "head")
    return jax.shard_map(body, mesh=mesh, in_specs=in_specs, out_specs=out_specs, check_vma=False)
```

```python
import functools

import jax
import jax.numpy as jnp
from jax import lax
from jax.experimental import pallas as pl
from jax.experimental.pallas import tpu as pltpu
from jax.sharding import PartitionSpec as P

HEAD_DIM = 128
CORES = 2
LOG2E = 1.4426950408889634
ANY = pl.BlockSpec(memory_space=pl.ANY)
HBM = pl.BlockSpec(memory_space=pltpu.HBM)
VMEM = pl.BlockSpec(memory_space=pltpu.VMEM)
SMEM = pl.BlockSpec(memory_space=pltpu.SMEM)
PARAMS = pltpu.CompilerParams(vmem_limit_bytes=16 * 2**20)
STACK_COST = pl.CostEstimate(flops=20 * 10**9, bytes_accessed=0, transcendentals=0)
NEAR_COST = pl.CostEstimate(flops=60 * 10**9, bytes_accessed=0, transcendentals=0)


def shifted(block, axis, distance):
    devices = range(lax.axis_size(axis))
    route = [((i - distance) % len(devices), i) for i in devices]
    return lax.ppermute(block, axis, route)


def swapped(block, axis, bits):
    route = [(i, i ^ bits) for i in range(lax.axis_size(axis))]
    return lax.ppermute(block, axis, route)


def place():
    me = lax.axis_index("seq")
    return me // CORES, me % CORES, lax.axis_index("head")


def over(block, turn):
    return swapped(block, "seq", CORES * turn)


def cut(start, size):
    return pl.ds(pl.multiple_of(start * size, size), size)


def copy_all(pairs, sem):
    copies = [pltpu.make_async_copy(one, other, sem.at[i]) for i, (one, other) in enumerate(pairs)]
    for at, one in enumerate(copies):
        one.start(priority=at % 2)
    return copies


def cut_pairs(k_ref, v_ref, chip, out):
    width = out.shape[1] // 2
    return [
        (k_ref.at[:, cut(chip, width)], out.at[:, pl.ds(0, width)]),
        (v_ref.at[:, cut(chip, width)], out.at[:, pl.ds(width, width)]),
    ]


def split_kernel(turns, q_ref, k_ref, v_ref, *rest):
    kv_refs, q_refs, sem = rest[: len(turns)], rest[len(turns) : -1], rest[-1]
    z, _, head = place()
    pairs = []
    for turn, out in zip(turns, kv_refs):
        pairs += cut_pairs(k_ref, v_ref, z ^ turn, out)
    for step, out in enumerate(q_refs, 1):
        pairs.append((q_ref.at[:, cut(head ^ step, out.shape[1])], out))
    for one in copy_all(pairs, sem):
        one.wait()


def split(queries, keys, values, turns, chips):
    rows, width = keys.shape
    others = queries.shape[1] // width - 1
    outs = [jax.ShapeDtypeStruct((rows, 2 * width // chips), keys.dtype)] * len(turns)
    outs += [jax.ShapeDtypeStruct((queries.shape[0], width), queries.dtype)] * others
    outs = pl.pallas_call(
        functools.partial(split_kernel, turns),
        out_shape=outs,
        in_specs=[HBM] * 3,
        out_specs=[ANY] * len(outs),
        scratch_shapes=[pltpu.SemaphoreType.DMA((2 * len(turns) + others,))],
        compiler_params=PARAMS,
    )(*in_hbm(queries, keys, values))
    return dict(zip(turns, outs)), outs[len(turns) :]


def in_hbm(*arrays):
    return [pltpu.with_memory_space_constraint(x, pltpu.HBM) for x in arrays]


def measure_kernel(turns, chips, order_ref, q_ref, k_ref, v_ref, _, *rest):
    kv_refs, q_out, rel_ref, sem = rest[: len(turns)], rest[-3], rest[-2], rest[-1]
    z, core, head = place()
    rows = k_ref.shape[0]
    pairs = [(q_ref.at[:, cut(head, q_out.shape[1])], q_out)]
    for turn, out in zip(turns, kv_refs):
        pairs += cut_pairs(k_ref, v_ref, z ^ turn, out)
    copies = copy_all(pairs, sem)
    inner = lax.broadcasted_iota(jnp.int32, (8, rows), 1)
    starts = [
        order_ref[(z ^ (slot % chips)) * CORES + (core ^ (slot // chips))] * rows for slot in range(chips * CORES)
    ]
    for turn in range(chips):
        for slot, start in enumerate(starts):
            rel_ref[turn, :, pl.ds(slot * rows, rows)] = inner + (start - starts[turn])
    for one in copies:
        one.wait()


def measure(block_order, queries, keys, values, turns, chips, after):
    rows, width = keys.shape
    outs = [jax.ShapeDtypeStruct((rows, 2 * width // chips), keys.dtype)] * len(turns)
    outs += [
        jax.ShapeDtypeStruct((queries.shape[0], width), queries.dtype),
        jax.ShapeDtypeStruct((chips, 8, rows * chips * CORES), jnp.int32),
    ]
    outs = pl.pallas_call(
        functools.partial(measure_kernel, turns, chips),
        out_shape=outs,
        in_specs=[SMEM] + [HBM] * 3 + [ANY],
        out_specs=[ANY] * (len(turns) + 1) + [VMEM],
        scratch_shapes=[pltpu.SemaphoreType.DMA((2 * len(turns) + 1,))],
        compiler_params=PARAMS,
    )(block_order, *in_hbm(queries, keys, values), after)
    return dict(zip(turns, outs)), outs[-2], outs[-1]


def regroup_kernel(groups, *refs):
    q_parts, q_refs = refs[:groups], refs[groups + 1 :]
    z, _, head = place()
    sub, (rows, width) = q_parts[0].shape[0], q_refs[0].shape
    for turn, out in enumerate(q_refs):
        for step, part in enumerate(q_parts):
            out[cut(head ^ step, sub), :] = part[:, cut(z ^ turn, width)]


def regroup(q_parts, rows, chips, after):
    return pl.pallas_call(
        functools.partial(regroup_kernel, len(q_parts)),
        out_shape=[jax.ShapeDtypeStruct((rows, q_parts[0].shape[1] // chips), q_parts[0].dtype)] * chips,
        in_specs=[VMEM] * len(q_parts) + [ANY],
        out_specs=[VMEM] * chips,
        compiler_params=PARAMS,
    )(*q_parts, after)


def stack_kernel(*refs):
    for at, ref in enumerate(refs[:-1]):
        refs[-1][at] = ref[...]


def stack(parts):
    return pl.pallas_call(
        stack_kernel,
        out_shape=jax.ShapeDtypeStruct((len(parts),) + parts[0].shape, parts[0].dtype),
        in_specs=[VMEM] * len(parts),
        out_specs=VMEM,
        compiler_params=PARAMS,
        cost_estimate=STACK_COST,
    )(*parts)


def attend_kernel(turns, count, first, last, stacked, alone, rel_ref, *rest):
    q_refs, rest = rest[: len(turns)], rest[len(turns) :]
    blocks, states, outs = [], (), ()
    if first:
        blocks, rest = list(rest[:count]), rest[count:]
    if last:
        others = {turn: rest[0].at[at] for at, turn in enumerate(stacked)} | dict(zip(alone, rest[1:]))
        blocks, rest = blocks + [others[turn] for turn in range(count)], rest[1 + len(alone) :]
        outs, rest = rest[len(rest) - len(turns) :], rest[: len(rest) - len(turns)]
    if not (first and last):
        states = rest[: 2 * len(turns)]
    rows, width = q_refs[0].shape
    scale = LOG2E / HEAD_DIM**0.5
    below = lax.broadcasted_iota(jnp.int32, (rows, CORES * rows), 0)
    ones = jnp.ones((CORES * rows, HEAD_DIM), jnp.bfloat16)
    start = 0 if first else count * rows

    def both(at, column):
        return jnp.concatenate([ref[:, pl.ds(column, HEAD_DIM)] for ref in blocks[at : at + CORES]], 0)

    for index, (turn, q_ref) in enumerate(zip(turns, q_refs)):
        top_ref, sums_ref = states[2 * index : 2 * index + 2] or (None, None)
        columns = range(0, width, HEAD_DIM)
        state = {column: None if first else (top_ref[:, pl.ds(column, HEAD_DIM)], sums_ref[:, pl.ds(2 * column, 2 * HEAD_DIM)]) for column in columns}
        for at in range(0, len(blocks), CORES):
            seen = rel_ref[turn, 0:1, pl.ds(start + at * rows, CORES * rows)] <= below
            for column in columns:
                s = lax.dot_general(
                    q_ref[:, pl.ds(column, HEAD_DIM)],
                    both(at, column),
                    (((1,), (1,)), ((), ())),
                    preferred_element_type=jnp.float32,
                )
                s = jnp.where(seen, s, jnp.float32(-1e30))
                high = jnp.broadcast_to(jnp.max(s, axis=1, keepdims=True), (rows, HEAD_DIM))
                if state[column] is not None:
                    top, sums = state[column]
                    high = jnp.maximum(top, high)
                weight = jnp.exp2((s - jnp.concatenate([high] * CORES, 1)) * scale).astype(jnp.bfloat16)
                values = jnp.concatenate([both(at, width + column), ones], 1)
                mixed = jnp.dot(weight, values, preferred_element_type=jnp.float32)
                if state[column] is not None:
                    shrink = jnp.exp2((top - high) * scale)
                    mixed += sums * jnp.concatenate([shrink, shrink], 1)
                state[column] = (high, mixed)
        for column, (top, sums) in state.items():
            if last:
                mean = sums[:, :HEAD_DIM] / sums[:, HEAD_DIM:]
                outs[index][:, pl.ds(column, HEAD_DIM)] = mean.astype(outs[index].dtype)
            else:
                top_ref[:, pl.ds(column, HEAD_DIM)] = top
                sums_ref[:, pl.ds(2 * column, 2 * HEAD_DIM)] = sums


def attend_near(turns, rel, q, near):
    rows, width = q[0].shape
    state = [jax.ShapeDtypeStruct((rows, wide), jnp.float32) for wide in (width, 2 * width)]
    outs = pl.pallas_call(
        functools.partial(attend_kernel, turns, len(near), True, False, (), ()),
        out_shape=state * len(turns),
        in_specs=[VMEM] * (1 + len(turns) + len(near)),
        out_specs=[VMEM] * (2 * len(turns)),
        compiler_params=PARAMS,
        cost_estimate=NEAR_COST,
    )(rel, *(q[turn] for turn in turns), *near)
    return {turn: outs[2 * index : 2 * index + 2] for index, turn in enumerate(turns)}


def attend(turns, rel, q, near, far, states, *after):
    stacked, swap, alone = far
    given = [*near, swap, *alone.values(), *(part for turn in turns for part in states.get(turn, ()))]
    outs = pl.pallas_call(
        functools.partial(attend_kernel, turns, len(q), bool(near), True, stacked, tuple(alone)),
        out_shape=[jax.ShapeDtypeStruct(q[0].shape, q[0].dtype)] * len(turns),
        in_specs=[VMEM] * (1 + len(turns) + len(given)) + [ANY] * len(after),
        out_specs=[VMEM] * len(turns),
        compiler_params=PARAMS,
    )(rel, *(q[turn] for turn in turns), *given, *after)
    return dict(zip(turns, outs))


def join_kernel(chips, *refs):
    parts, out = refs[:chips], refs[-1]
    z, _, _ = place()
    width = parts[0].shape[1]
    for turn, part in enumerate(parts):
        out[:, cut(z ^ turn, width)] = part[...]


def join(parts):
    chips, (rows, width) = len(parts), parts[0].shape
    return pl.pallas_call(
        functools.partial(join_kernel, chips),
        out_shape=jax.ShapeDtypeStruct((rows, width * chips), parts[0].dtype),
        in_specs=[VMEM] * chips,
        out_specs=VMEM,
        compiler_params=PARAMS,
    )(*parts)


def by_heads(queries, keys, values, block_order):
    chips = lax.axis_size("seq") // CORES
    groups = lax.axis_size("head")
    half = chips // 2
    across, within = list(range(half, chips)), list(range(1, half))
    kv, q_cut = split(queries, keys, values, [*across[::-1], *within], chips)
    q_parts = [swapped(part, "head", step) for step, part in enumerate(q_cut, 1)]
    kv_late, q_own, rel = measure(block_order, queries, keys, values, [0], chips, q_parts[0])
    kv |= kv_late
    near = [kv[0]] + [over(kv[turn], turn) for turn in range(1, chips)]
    q = regroup([q_own, *q_parts], keys.shape[0], chips, rel)
    q = [q[0]] + [over(q[turn], turn) for turn in range(1, chips)]
    stacked = [*across[::-1], 0]
    swap = swapped(stack([near[turn] for turn in stacked]), "seq", 1)
    far = (stacked, swap, {turn: swapped(near[turn], "seq", 1) for turn in within})
    states = attend_near([0, *within], rel, q, near)
    done = attend(within, rel, q, (), far, states) if within else {}
    out = {turn: over(part, turn) for turn, part in done.items()}
    for turn in across[::-1]:
        out[turn] = over(attend([turn], rel, q, near, far, {}, *done.values())[turn], turn)
    out |= attend([0], rel, q, (), far, states)
    return join([out[turn] for turn in range(chips)])


def around_ring(queries, keys, values, block_order):
    seq_count = lax.axis_size("seq")
    me_index = lax.axis_index("seq")
    local_q = lax.all_to_all(queries, "head", split_axis=1, concat_axis=0, tiled=True)
    rows = local_q.shape[0]
    head_count = local_q.shape[1] // HEAD_DIM
    q_three = local_q.reshape(rows, head_count, HEAD_DIM)
    mine = block_order[me_index]
    scale = 1.0 / HEAD_DIM**0.5

    def tile(state, kv_pair, allowed):
        rowmax, total, accum = state
        key_count = kv_pair[0].shape[0]
        k_three = kv_pair[0].reshape(key_count, head_count, HEAD_DIM)
        v_three = kv_pair[1].reshape(key_count, head_count, HEAD_DIM)
        scores = (
            jnp.einsum("qhd,khd->hqk", q_three, k_three, preferred_element_type=jnp.float32) * scale
        )
        scores = jnp.where(allowed[None], scores, jnp.float32(-1e30))
        new_max = jnp.maximum(rowmax, jnp.max(scores, axis=2))
        factor = jnp.exp(rowmax - new_max)
        weight = jnp.where(allowed[None], jnp.exp(scores - new_max[:, :, None]), jnp.float32(0.0))
        total = total * factor + jnp.sum(weight, axis=2)
        mixed = jnp.einsum(
            "hqk,khd->qhd", weight.astype(jnp.bfloat16), v_three, preferred_element_type=jnp.float32
        )
        accum = accum * jnp.transpose(factor)[:, :, None] + mixed
        return (new_max, total, accum)

    def absorb(state, kv_pair, source):
        visible = block_order[source % seq_count] < mine
        allowed = jnp.broadcast_to(visible, (rows, rows))
        return tile(state, kv_pair, allowed)

    start_state = (
        jnp.full((head_count, rows), -1e30, jnp.float32),
        jnp.zeros((head_count, rows), jnp.float32),
        jnp.zeros((rows, head_count, HEAD_DIM), jnp.float32),
    )
    query_idx = lax.broadcasted_iota(jnp.int32, (rows, rows), 0)
    key_idx = lax.broadcasted_iota(jnp.int32, (rows, rows), 1)
    state = tile(start_state, (keys, values), key_idx <= query_idx)

    def both_turn(step, carry):
        ahead, behind, st = carry
        ahead = tuple(shifted(part, "seq", 1) for part in ahead)
        st = absorb(st, ahead, me_index - step + seq_count)
        behind = tuple(shifted(part, "seq", -1) for part in behind)
        st = absorb(st, behind, me_index + step)
        return (ahead, behind, st)

    ahead, behind, state = lax.fori_loop(
        1, (seq_count - 1) // 2 + 1, both_turn, ((keys, values), (keys, values), state)
    )
    if seq_count % 2 == 0:
        ahead = tuple(shifted(part, "seq", 1) for part in ahead)
        state = absorb(state, ahead, me_index - seq_count // 2 + seq_count)
    rowmax, total, accum = state
    result = accum / jnp.transpose(total)[:, :, None]
    return result.reshape(rows, head_count * HEAD_DIM).astype(jnp.bfloat16)


def body(queries, keys, values, block_order):
    seq_count, groups = lax.axis_size("seq"), lax.axis_size("head")
    chips = seq_count // CORES
    heads = keys.shape[1] // HEAD_DIM
    powers = all(n > 1 and n & (n - 1) == 0 for n in (chips, groups))
    if seq_count % CORES == 0 and powers and heads % chips == 0:
        return by_heads(queries, keys, values, block_order)
    return around_ring(queries, keys, values, block_order)


def solution(mesh):
    in_specs = (P(("seq", "head"), None), P("seq", "head"), P("seq", "head"), P())
    out_specs = P("seq", "head")
    return jax.shard_map(body, mesh=mesh, in_specs=in_specs, out_specs=out_specs, check_vma=False)
```
